256 devices in a mesh: blk: 64 (over y, z, x_hi), rank: 4 (over x_lo, core).
Axes of the slice: x: 4 (x_hi: 2, x_lo: 2; x = x_hi * 2 + x_lo), y: 4, z: 8, core: 2. Of those that a mesh axis runs over, the one named last changes fastest.
Arguments:
- ratings: bfloat16 [4096, 128, 128], P('blk'), may hold values from -6 to 6
- send_list: int32 [64, 64], P('blk'), may hold values from 0 to 63, each once within a row
- plan: int32 [64, 64], P('blk'), may hold values from 0 to 63, each once within a row
- block_count: int32 [64, 4], P('blk'), may hold values from 8 to 16, as said below
- block_user: int32 [64, 64], P('blk'), may hold values from 0 to 7
- block_item: int32 [64, 64], P('blk'), may hold values from 0 to 3
- user_factors: float32 [256, 65536], P('rank', 'blk'), may hold values from -1.5 to 1.5
- item_factors: float32 [256, 32768], P('rank', 'blk'), may hold values from -1.5 to 1.5
- item_accum: float32 [256, 32768], P('rank', 'blk'), may hold values from 1 to 16
Outputs:
- users_out: float32 [256, 65536], P('rank', 'blk')
- items_out: float32 [256, 32768], P('rank', 'blk')
- accum_out: float32 [256, 32768], P('rank', 'blk')
The draws below stay inside these ranges and needn't reach their ends.
Inputs may be any that keep to these rules, and one draw needn't show every extreme that they name: `block_count`: every owner has at least 8 live slots in each stratum; in every draw some owner has 16 live slots in every stratum.
All inputs are finite; a program needn't handle non-finite values.
Results may differ from the reference program's by a relative error of at most 0.0003.
Values may be sent and summed in bfloat16 or wider, within the bound.
No kernel may reach another device: no remote copies, remote signals or barrier semaphores. Data moves between devices by JAX's collectives and lax.ppermute only.
A program may use at most 64 MiB of HBM per device.

```python
import math
import jax
import jax.numpy as jnp
from jax import lax

R = 256
BS = 128
UB_DEV = 8
IB_DEV = 4
STRATA = 4
PER_S = 16
NB_DEV = 64
NB_ALL = 4096
USERS = 65536
ITEMS = 32768
N_BLK = 64


def draw_block_count(key, part):
    key = jax.random.fold_in(key, 5)
    first, second, third = jax.random.split(key, 3)
    light = jax.random.randint(first, (N_BLK, STRATA), PER_S // 2, PER_S + 1)
    heavy = jax.random.randint(second, (N_BLK, 1), 0, 8) == 0
    forced = jax.random.randint(third, (), 0, N_BLK)
    heavy = heavy | (jnp.arange(N_BLK)[:, None] == forced)
    return jnp.where(heavy, PER_S, light).astype(jnp.int32)


def touch_ends(drawn, rng, smallest, high):
    shape = drawn.shape
    place = [jax.random.randint(jax.random.fold_in(rng, axis), (), 0, shape[axis]) for axis in range(len(shape))]
    drawn = drawn.at[tuple(place)].set(smallest)
    longest = shape.index(max(shape))
    place[longest] = (place[longest] + 1) % shape[longest]
    return drawn.at[tuple(place)].set(high)


def shard_levels(key, extent, cuts, smallest, top_value):
    def one(dim, blocks):
        heights = jax.random.uniform(jax.random.fold_in(jax.random.fold_in(key, 6), dim), (blocks,), jnp.float32, smallest / len(cuts), top_value / len(cuts))
        return jnp.repeat(jnp.exp(heights), extent[dim] // blocks).reshape((-1,) + (1,) * (len(extent) - dim - 1))

    loudness = one(*cuts[0])
    for cut in cuts[1:]:
        loudness = loudness * one(*cut)
    return loudness


def gaussian(rng, shape, spread, most, pieces=(), held_as=jnp.bfloat16):
    drawn = spread * jax.random.normal(rng, shape, jnp.float32)
    if pieces:
        drawn = drawn * shard_levels(rng, shape, pieces, -0.22, 0.18)
    return jnp.clip(drawn, -most, most).astype(held_as)


def setup_inputs(seed: int = 0) -> dict:
    streams_of = jax.random.split(jax.random.key(seed), 10)
    return {
        "ratings": gaussian(streams_of[0], (NB_ALL, BS, BS), 1.0, 6.0, ((0, 64),)),
        "send_list": jax.vmap(lambda own: jax.random.permutation(own, NB_DEV))(jax.random.split(streams_of[1], N_BLK)).reshape((N_BLK, NB_DEV)).astype(jnp.int32),
        "plan": jax.vmap(lambda own: jax.random.permutation(own, NB_DEV))(jax.random.split(streams_of[2], N_BLK)).reshape((N_BLK, NB_DEV)).astype(jnp.int32),
        "block_count": draw_block_count(jax.random.fold_in(streams_of[9], 71), 0),
        "block_user": touch_ends(jax.random.randint(streams_of[4], (N_BLK, NB_DEV), 0, UB_DEV), jax.random.fold_in(streams_of[4], 1), 0, UB_DEV - 1).astype(jnp.int32),
        "block_item": touch_ends(jax.random.randint(streams_of[5], (N_BLK, NB_DEV), 0, IB_DEV), jax.random.fold_in(streams_of[5], 1), 0, IB_DEV - 1).astype(jnp.int32),
        "user_factors": gaussian(streams_of[6], (R, USERS), 0.25, 1.5, ((0, 4), (1, 64)), jnp.float32),
        "item_factors": gaussian(streams_of[7], (R, ITEMS), 0.25, 1.5, ((0, 4), (1, 64)), jnp.float32),
        "item_accum": jnp.clip(jnp.exp(math.log(16.0) - 2.7725887 * jax.random.uniform(streams_of[8], (R, ITEMS), jnp.float32) ** shard_levels(streams_of[8], (R, ITEMS), ((0, 4), (1, 64)), -0.2, 0.2)), 1.0, 16.0),
    }


HIGH = lax.Precision.HIGHEST
LR_USER = 0.01
LR_ITEM = 0.05
DECAY = 0.05

def apply_stratum(received, slot_ids, counts_now, user_ids, item_ids, users, items, accum):
    tiles_now = received[slot_ids].astype(jnp.float32)
    active = (jnp.arange(PER_S, dtype=jnp.int32) < counts_now).astype(jnp.float32)
    pick_user = (user_ids[:, None] == jnp.arange(UB_DEV, dtype=jnp.int32)[None, :]).astype(jnp.float32)
    pick_item = (item_ids[:, None] == jnp.arange(IB_DEV, dtype=jnp.int32)[None, :]).astype(jnp.float32)
    user_rows = jnp.einsum('pu,run->prn', pick_user, users, precision=HIGH)
    item_rows = jnp.einsum('pi,rim->prm', pick_item, items, precision=HIGH)
    predicted = jnp.einsum('prn,prm->pnm', user_rows, item_rows, precision=HIGH)
    errors = active[:, None, None] * (tiles_now - predicted)
    user_terms = jnp.einsum('pnm,prm->prn', errors, item_rows, precision=HIGH)
    item_terms = jnp.einsum('pnm,prn->prm', errors, user_rows, precision=HIGH)
    grad_user = jnp.einsum('pu,prn->run', pick_user, user_terms, precision=HIGH) - DECAY * users
    grad_item = jnp.einsum('pi,prm->rim', pick_item, item_terms, precision=HIGH) - DECAY * items
    users = users + LR_USER * grad_user
    accum = accum + grad_item * grad_item
    items = items + LR_ITEM * grad_item / jnp.sqrt(accum)
    return (users, items, accum)

def reference(ratings, send_list, plan, block_count, block_user, block_item, user_factors, item_factors, item_accum):
    per_peer = STRATA * PER_S // N_BLK
    stacked = ratings.reshape(N_BLK, NB_DEV, BS, BS)
    routes = send_list.reshape(N_BLK, N_BLK, per_peer)
    sources = jnp.arange(N_BLK, dtype=jnp.int32)[:, None, None]
    outgoing = stacked[sources, routes]
    received = jnp.swapaxes(outgoing, 0, 1).reshape(N_BLK, NB_DEV, BS, BS)
    users = user_factors.reshape(R, N_BLK, UB_DEV, BS).transpose(1, 0, 2, 3)
    items = item_factors.reshape(R, N_BLK, IB_DEV, BS).transpose(1, 0, 2, 3)
    accum = item_accum.reshape(R, N_BLK, IB_DEV, BS).transpose(1, 0, 2, 3)
    plan_all = plan.reshape(N_BLK, STRATA, PER_S)
    user_all = block_user.reshape(N_BLK, STRATA, PER_S)
    item_all = block_item.reshape(N_BLK, STRATA, PER_S)
    for stratum in range(STRATA):
        users, items, accum = jax.vmap(apply_stratum)(received, plan_all[:, stratum], block_count[:, stratum], user_all[:, stratum], item_all[:, stratum], users, items, accum)
        items = jnp.roll(items, 1, axis=0)
        accum = jnp.roll(accum, 1, axis=0)
    users_out = users.transpose(1, 0, 2, 3).reshape(R, USERS)
    items_out = items.transpose(1, 0, 2, 3).reshape(R, ITEMS)
    accum_out = accum.transpose(1, 0, 2, 3).reshape(R, ITEMS)
    return (users_out, items_out, accum_out)
```

```python
import functools

import jax
import jax.numpy as jnp
from jax import lax
from jax.experimental import pallas as pl
from jax.experimental.pallas import tpu as pltpu
from jax.sharding import PartitionSpec as P

LR_USER = 0.01
LR_ITEM = 0.05
DECAY = 0.05
F32 = jnp.float32
BF16 = jnp.bfloat16
EDGE = 128
SLOTS = 16
STRATA = 4
QUARTER = 32
CHUNK = 256
VMEM = pl.BlockSpec(memory_space=pltpu.VMEM)
SMEM = pl.BlockSpec(memory_space=pltpu.SMEM)
ANY = pl.BlockSpec(memory_space=pl.ANY)
PARAMS = pltpu.CompilerParams(vmem_limit_bytes=40 * 2**20)


def cost(flops, bytes_accessed):
    return pl.CostEstimate(flops=flops, bytes_accessed=bytes_accessed, transcendentals=0)


def split(x):
    high = x.astype(BF16)
    return high, (x - high.astype(F32)).astype(BF16)


def dot(a, b):
    return jnp.dot(a, b, preferred_element_type=F32)


def dot_nt(a, b):
    return lax.dot_general(a, b, (((1,), (1,)), ((), ())), preferred_element_type=F32)


def three(product, a, b):
    return product(a[0], b[0]) + product(a[0], b[1]) + product(a[1], b[0])


def struct(*shape, dtype=F32):
    return jax.ShapeDtypeStruct(shape, dtype)


def gather_kernel(rank, routes, ratings, out, sem):
    row = pl.multiple_of(rank[0] * QUARTER, QUARTER)

    def copy(d):
        return pltpu.make_async_copy(
            ratings.at[routes[0, d], pl.ds(row, QUARTER), :], out.at[d], sem
        )

    for d in range(64):
        copy(d).start()
    pltpu.make_async_copy(out, out, sem).wait()


def gather_outgoing(rank, routes, ratings):
    return pl.pallas_call(
        gather_kernel,
        out_shape=struct(64, QUARTER, EDGE, dtype=BF16),
        in_specs=[SMEM, SMEM, ANY],
        out_specs=ANY,
        scratch_shapes=[pltpu.SemaphoreType.DMA],
        compiler_params=PARAMS,
        cost_estimate=cost(0, 2**20),
        name="gather_outgoing",
    )(rank, routes, ratings)


def order_kernel(plan, received, first, rest):
    for p in range(SLOTS):
        first[p] = received[plan[0, p]]
    for p in range(SLOTS, STRATA * SLOTS):
        rest[p - SLOTS] = received[plan[0, p]]


def order_received(plan, received):
    return pl.pallas_call(
        order_kernel,
        out_shape=(
            struct(SLOTS, QUARTER, EDGE, dtype=BF16),
            struct(3 * SLOTS, QUARTER, EDGE, dtype=BF16),
        ),
        in_specs=[SMEM, VMEM],
        out_specs=(VMEM, VMEM),
        compiler_params=PARAMS,
        cost_estimate=cost(0, 2**20),
        name="order_received",
    )(plan, received)


def store_users(uf, first, last, uf_ref, uh, ul, uth, utl):
    cols = slice(first, last)
    high, low = split(uf)
    uf_ref[:, cols] = uf
    uh[:, cols] = high
    ul[:, cols] = low
    turned = uf.T
    high, low = split(turned)
    uth[cols, :] = high
    utl[cols, :] = low


def prepare_kernel(own, pair, sib, uf, uh, ul, uth, utl):
    for first in range(0, 1024, CHUNK):
        cols = slice(first, first + CHUNK)
        part = jnp.concatenate(
            [own[:, cols], pair[:, cols], sib[0, :, cols], sib[1, :, cols]], axis=0
        )
        store_users(part, first, first + CHUNK, uf, uh, ul, uth, utl)


USER_SHAPES = (
    struct(256, 1024),
    struct(256, 1024, dtype=BF16),
    struct(256, 1024, dtype=BF16),
    struct(1024, 256, dtype=BF16),
    struct(1024, 256, dtype=BF16),
)


def prepare_users(own, pair, sib):
    return pl.pallas_call(
        prepare_kernel,
        out_shape=USER_SHAPES,
        in_specs=[VMEM] * 3,
        out_specs=(VMEM,) * 5,
        compiler_params=PARAMS,
        cost_estimate=cost(2**20, 4 * 2**20),
        name="prepare_users",
    )(own, pair, sib)


def add_tiles(stratum, half, rank, count, user, item, pieces, sums):
    sums[...] = jnp.zeros_like(sums)
    live = count[0, stratum]
    base = 0 if stratum == 0 else (stratum - 1) * SLOTS
    own, pair, sib = pieces
    for p in range(SLOTS):
        slot = stratum * SLOTS + p
        block = item[0, slot]

        @pl.when((p < live) & (block // 2 == half))
        def _():
            top = user[0, slot] * EDGE
            for k, piece in enumerate((own, pair, sib.at[0], sib.at[1])):
                quarter = rank ^ (0, 2, 1, 3)[k]
                rows = pl.ds(pl.multiple_of(top + quarter * QUARTER, QUARTER), QUARTER)
                sums[block % 2, rows, :] += piece[base + p].astype(F32)


def errors(stratum, half, first, counts, predicted, sums):
    rows = []
    for r in range(CHUNK // EDGE):
        start = first + r * EDGE
        columns = []
        for c in range(2):
            live = counts[stratum, (start // EDGE) * 4 + half * 2 + c]
            columns.append(
                sums[c, start : start + EDGE, :]
                - live * predicted[r * EDGE : (r + 1) * EDGE, c * EDGE : (c + 1) * EDGE]
            )
        rows.append(jnp.concatenate(columns, axis=1))
    return jnp.concatenate(rows, axis=0)


def item_kernel(
    stratum, rank, count, user, item, counts, uh, ul, uth, utl, v, a, own, pair, sib, *rest
):
    *outs, eh, el, sums = rest
    half = rank[0] % 2
    add_tiles(stratum, half, rank[0], count, user, item, (own, pair, sib), sums)
    items = v[...]
    vs = split(items)
    grad = jnp.zeros_like(items)
    for first in range(0, 1024, CHUNK):
        rows = slice(first, first + CHUNK)
        predicted = three(dot, (uth[rows, :], utl[rows, :]), vs)
        es = split(errors(stratum, half, first, counts, predicted, sums))
        eh[rows, :], el[rows, :] = es
        grad += three(dot, (uh[:, rows], ul[:, rows]), es)
    grad = grad - DECAY * items
    accum = a[...] + grad * grad
    items = items + LR_ITEM * grad / jnp.sqrt(accum)
    if stratum < STRATA - 1:
        outs[0][...] = items
        outs[1][...] = accum
    else:
        for k in range(2):
            outs[k][0] = items[k * 128 : k * 128 + 64]
            outs[k][1] = accum[k * 128 : k * 128 + 64]


def item_step(stratum, scalars, users, v, a, pieces):
    if stratum < STRATA - 1:
        out = (struct(256, 256), struct(256, 256))
    else:
        out = (struct(2, 64, 256), struct(2, 64, 256))
    return pl.pallas_call(
        functools.partial(item_kernel, stratum),
        out_shape=out + (struct(1024, 256, dtype=BF16), struct(1024, 256, dtype=BF16)),
        in_specs=[SMEM] * 5 + [VMEM] * 9,
        out_specs=(VMEM,) * 4,
        scratch_shapes=[pltpu.VMEM((2, 1024, EDGE), F32)],
        compiler_params=PARAMS,
        cost_estimate=cost(10**9, 4 * 2**20),
        name=f"item_step{stratum}",
    )(*scalars, *users[1:], v, a, *pieces)


def user_kernel(
    stratum,
    rank,
    count,
    user,
    item,
    counts,
    uf,
    uth,
    utl,
    v,
    vo,
    eh,
    el,
    own,
    pair,
    sib,
    *rest,
):
    *outs, sums = rest
    half = 1 - rank[0] % 2
    add_tiles(stratum, half, rank[0], count, user, item, (own, pair, sib), sums)
    kept = 256 if stratum < STRATA - 1 else 64
    vs = split(v[:kept, :])
    vos = split(jnp.concatenate([vo[128:, :], vo[:128, :]], axis=0))
    for first in range(0, 1024, CHUNK):
        rows = slice(first, first + CHUNK)
        predicted = three(dot, (uth[rows, :], utl[rows, :]), vos)
        es = split(errors(stratum, half, first, counts, predicted, sums))
        grad = three(dot_nt, vs, (eh[rows, :], el[rows, :]))
        grad += three(dot_nt, (vos[0][:kept], vos[1][:kept]), es)
        old = uf[:kept, rows]
        new = old + LR_USER * (grad - DECAY * old)
        if stratum < STRATA - 1:
            store_users(new, first, first + CHUNK, *outs)
        else:
            outs[0][:, rows] = new


def user_step(stratum, scalars, users, v, vo, es, pieces):
    last = stratum == STRATA - 1
    return pl.pallas_call(
        functools.partial(user_kernel, stratum),
        out_shape=(struct(64, 1024),) if last else USER_SHAPES,
        in_specs=[SMEM] * 5 + [VMEM] * 10,
        out_specs=(VMEM,) * (1 if last else 5),
        scratch_shapes=[pltpu.VMEM((2, 1024, EDGE), F32)],
        compiler_params=PARAMS,
        cost_estimate=cost(2 * 10**9, 6 * 2**20),
        name=f"user_step{stratum}",
    )(*scalars, users[0], users[3], users[4], v, vo, *es, *pieces)


def exchange(x, by):
    return lax.ppermute(x, "rank", [(r, r ^ by) for r in range(4)])


def send_on(x, by):
    n = lax.axis_size("blk")
    return lax.ppermute(
        x,
        ("blk", "rank"),
        [(o * 4 + r, (o + 1) % n * 4 + (r ^ by)) for o in range(n) for r in range(4)],
    )


def gather_group(own):
    pair = exchange(own, 2)
    return own, pair, exchange(jnp.stack([own, pair]), 1)


def body(
    ratings,
    send_list,
    plan,
    block_count,
    block_user,
    block_item,
    user_factors,
    item_factors,
    item_accum,
):
    index = lax.axis_index("rank").astype(jnp.int32)
    rank = index.reshape(1)
    core = index % 2

    pair_users = exchange(user_factors, 2)
    state = jnp.stack([item_factors, item_accum])
    pair_state = exchange(state, 2)

    outgoing = gather_outgoing(rank, send_list, ratings)
    received = lax.all_to_all(outgoing, "blk", split_axis=0, concat_axis=0, tiled=True)

    sib_users = exchange(jnp.stack([user_factors, pair_users]), 1)
    users = prepare_users(user_factors, pair_users, sib_users)
    both = jnp.stack([state, pair_state], axis=1).reshape(2, 2, 64, 2, 256)
    mine = lax.dynamic_index_in_dim(both, core, 3, keepdims=False)
    others = exchange(lax.dynamic_index_in_dim(both, 1 - core, 3, keepdims=False), 1)
    held = jnp.concatenate([mine, others], axis=1).reshape(2, 256, 256)
    v, a = held[0], held[1]

    active = jnp.arange(SLOTS, dtype=jnp.int32)[None, :] < block_count.reshape(STRATA, 1)
    place = (block_user * 4 + block_item).reshape(STRATA, SLOTS)
    hits = place[:, :, None] == jnp.arange(32, dtype=jnp.int32)
    counts = jnp.sum((hits & active[:, :, None]).astype(F32), axis=1)
    scalars = (rank, block_count, block_user, block_item, counts)

    first, rest = order_received(plan, received)
    pieces = gather_group(first)
    for stratum in range(STRATA):
        *out, eh, el = item_step(stratum, scalars, users, v, a, pieces)
        if stratum < STRATA - 1:
            v_next = send_on(out[0], 0)
            a_next = send_on(out[1], 0)
        else:
            near = send_on(out[0], 0)
            far = send_on(out[1], 1)
        if stratum == 0:
            rest, eh = lax.optimization_barrier((rest, eh))
            pieces_next = gather_group(rest)
        vo = exchange(v, 1)
        users = user_step(stratum, scalars, users, v, vo, (eh, el), pieces)
        if stratum == 0:
            pieces = pieces_next
        if stratum < STRATA - 1:
            v, a = v_next, a_next
    low = jnp.where(core == 0, near, far)
    high = jnp.where(core == 0, far, near)
    moved = jnp.concatenate([low, high], axis=2)
    return users[0], moved[0], moved[1]


def solution(mesh):
    placed = (
        P("blk", None, None),
        P("blk", None),
        P("blk", None),
        P("blk", None),
        P("blk", None),
        P("blk", None),
        P("rank", "blk"),
        P("rank", "blk"),
        P("rank", "blk"),
    )
    return jax.shard_map(
        body,
        mesh=mesh,
        in_specs=placed,
        out_specs=(P("rank", "blk"), P("rank", "blk"), P("rank", "blk")),
        check_vma=False,
    )
```

```python
import functools

import jax
import jax.numpy as jnp
from jax import lax
from jax.experimental import pallas as pl
from jax.experimental.pallas import tpu as pltpu
from jax.sharding import PartitionSpec as P

LR_USER = 0.01
LR_ITEM = 0.05
DECAY = 0.05
F32 = jnp.float32
BF16 = jnp.bfloat16
EDGE = 128
SLOTS = 16
STRATA = 4
QUARTER = 32
CHUNK = 256
VMEM = pl.BlockSpec(memory_space=pltpu.VMEM)
SMEM = pl.BlockSpec(memory_space=pltpu.SMEM)
ANY = pl.BlockSpec(memory_space=pl.ANY)
PARAMS = pltpu.CompilerParams(vmem_limit_bytes=16 * 2**20)


def cost(time):
    return pl.CostEstimate(flops=10**9 * time, bytes_accessed=3 * 10**6 * time, transcendentals=0)


def split(x):
    high = x.astype(BF16)
    return high, (x - high.astype(F32)).astype(BF16)


def dot(a, b):
    return jnp.dot(a, b, preferred_element_type=F32)


def dot_nt(a, b):
    return lax.dot_general(a, b, (((1,), (1,)), ((), ())), preferred_element_type=F32)


def three(product, a, b):
    return product(a[0], b[0]) + product(a[0], b[1]) + product(a[1], b[0])


def struct(*shape, dtype=F32):
    return jax.ShapeDtypeStruct(shape, dtype)


def gather_kernel(rank, routes, count, user, item, ratings, out, counts, sem):
    row = pl.multiple_of(rank[0] * QUARTER, QUARTER)
    for d in range(64):
        pltpu.make_async_copy(
            ratings.at[routes[0, d], pl.ds(row, QUARTER), :], out.at[d], sem
        ).start()
    for s in range(STRATA):
        for k in range(32):
            counts[s, k] = 0.0
        for p in range(SLOTS):
            slot = s * SLOTS + p
            where = user[0, slot] * 4 + item[0, slot]
            counts[s, where] += jnp.where(p < count[0, s], 1.0, 0.0)
    pltpu.make_async_copy(out, out, sem).wait()


def gather_outgoing(rank, routes, count, user, item, ratings):
    return pl.pallas_call(
        gather_kernel,
        out_shape=(struct(64, QUARTER, EDGE, dtype=BF16), struct(STRATA, 32)),
        in_specs=[SMEM] * 5 + [ANY],
        out_specs=(VMEM, SMEM),
        scratch_shapes=[pltpu.SemaphoreType.DMA],
        compiler_params=PARAMS,
        cost_estimate=cost(2),
        name="gather_outgoing",
    )(rank, routes, count, user, item, ratings)


def order_kernel(plan, received, first, rest):
    for p in range(SLOTS):
        first[p] = received[plan[0, p]]
    for p in range(SLOTS, STRATA * SLOTS):
        rest[p - SLOTS] = received[plan[0, p]]


def order_received(plan, received):
    return pl.pallas_call(
        order_kernel,
        out_shape=(
            struct(SLOTS, QUARTER, EDGE, dtype=BF16),
            struct(3 * SLOTS, QUARTER, EDGE, dtype=BF16),
        ),
        in_specs=[SMEM, VMEM],
        out_specs=(VMEM, VMEM),
        compiler_params=PARAMS,
        cost_estimate=cost(4),
        name="order_received",
    )(plan, received)


def store_users(uf, first, last, uf_ref, uh, ul, uth, utl):
    cols = slice(first, last)
    high, low = split(uf)
    uf_ref[:, cols] = uf
    uh[:, cols] = high
    ul[:, cols] = low
    turned = uf.T
    high, low = split(turned)
    uth[cols, :] = high
    utl[cols, :] = low


def group_rows(rank):
    return [pl.ds(pl.multiple_of((rank ^ k) * 64, 64), 64) for k in (0, 2, 1, 3)]


def block_of(ref, rank, base):
    return ref[:, pl.ds(pl.multiple_of(base + rank * EDGE, EDGE), EDGE)]


def pack_kernel(rank, users, items, accum, pair, out):
    sibling = rank[0] ^ 1
    out[0, :, :1024] = users[...]
    out[1, :, :1024] = pair[:, :1024]
    out[0, :, 1024 : 1024 + EDGE] = block_of(items, sibling, 0)
    out[0, :, 1024 + EDGE :] = block_of(accum, sibling, 0)
    out[1, :, 1024 : 1024 + EDGE] = block_of(pair, sibling, 1024)
    out[1, :, 1024 + EDGE :] = block_of(pair, sibling, 1536)


def pack(rank, users, items, accum, pair):
    return pl.pallas_call(
        pack_kernel,
        out_shape=struct(2, 64, 1280),
        in_specs=[SMEM] + [VMEM] * 4,
        out_specs=VMEM,
        compiler_params=PARAMS,
        cost_estimate=cost(4),
        name="pack",
    )(rank, users, items, accum, pair)


def prepare_kernel(
    rank, own, items, accum, pair, sib, uf, uh, ul, uth, utl, state, users
):
    mine = rank[0]
    places = group_rows(mine)
    parts = (own, pair.at[:, :1024], sib.at[0, :, :1024], sib.at[1, :, :1024])
    for place, part in zip(places, parts):
        users[place, :] = part[...]
    for first in range(0, 1024, CHUNK):
        last = first + CHUNK
        store_users(users[:, first:last], first, last, uf, uh, ul, uth, utl)
    for k, own_part in enumerate((items, accum)):
        state[k, places[0], :] = block_of(own_part, mine, 0)
        state[k, places[1], :] = block_of(pair, mine, 1024 + 512 * k)
        for j in range(2):
            start = 1024 + EDGE * k
            state[k, places[2 + j], :] = sib[j, :, start : start + EDGE]


USER_SHAPES = (
    struct(256, 1024),
    struct(256, 1024, dtype=BF16),
    struct(256, 1024, dtype=BF16),
    struct(1024, 256, dtype=BF16),
    struct(1024, 256, dtype=BF16),
)


def prepare(rank, own, items, accum, pair, sib):
    return pl.pallas_call(
        prepare_kernel,
        out_shape=USER_SHAPES + (struct(2, 256, EDGE),),
        in_specs=[SMEM] + [VMEM] * 5,
        out_specs=(VMEM,) * 6,
        scratch_shapes=[pltpu.VMEM((256, 1024), F32)],
        compiler_params=PARAMS,
        cost_estimate=cost(12),
        name="prepare",
    )(rank, own, items, accum, pair, sib)


def add_tile(rank, place, pieces, top, sums):
    own, pair, sib = pieces
    for k, piece in zip((0, 2, 1, 3), (own, pair, sib.at[0], sib.at[1])):
        start = pl.multiple_of(top + (rank ^ k) * QUARTER, QUARTER)
        sums[pl.ds(start, QUARTER), :] += piece[place].astype(F32)


def item_kernel(
    stratum, rank, count, user, item, counts, uh, ul, uth, utl, state, own, pair, sib, *rest
):
    *outs, errors, sums = rest
    mine = rank[0]
    sums[...] = jnp.zeros_like(sums)
    for p in range(SLOTS):
        slot = stratum * SLOTS + p

        @pl.when((p < count[0, stratum]) & (item[0, slot] == mine))
        def _():
            place = p if stratum == 0 else slot - SLOTS
            add_tile(mine, place, (own, pair, sib), user[0, slot] * EDGE, sums)

    items = state[0]
    vh, vl = split(items)
    both = jnp.concatenate([vh, vl], axis=1)
    grad = jnp.zeros_like(items)
    for first in range(0, 1024, CHUNK):
        rows = slice(first, first + CHUNK)
        wide = dot(uth[rows, :], both)
        predicted = wide[:, :EDGE] + wide[:, EDGE:] + dot(utl[rows, :], vh)
        parts = []
        for k in range(CHUNK // EDGE):
            top = first + k * EDGE
            live = counts[stratum, top // EDGE * 4 + mine]
            parts.append(sums[top : top + EDGE, :] - live * predicted[k * EDGE : (k + 1) * EDGE])
        eh, el = split(jnp.concatenate(parts, axis=0))
        es = jnp.concatenate([eh, el], axis=1)
        errors[rows, :] = es
        wide = dot(uh[:, rows], es)
        grad += wide[:, :EDGE] + wide[:, EDGE:] + dot(ul[:, rows], eh)
    grad = grad - DECAY * items
    accum = state[1] + grad * grad
    items = items + LR_ITEM * grad / jnp.sqrt(accum)
    if stratum < STRATA - 1:
        outs[0][0] = items
        outs[0][1] = accum
    else:
        kept, passed, spot = outs[0], outs[1], outs[2]
        spot[0] = items
        spot[1] = accum
        for j, rows in enumerate(group_rows(mine)):
            target = kept if j < 2 else passed
            for k in range(2):
                target[j % 2, k] = spot[k, rows, :]


def item_step(stratum, scalars, users, state, pieces):
    scratch = [pltpu.VMEM((1024, EDGE), F32)]
    if stratum < STRATA - 1:
        out = (struct(2, 256, EDGE),)
    else:
        out = (struct(2, 2, 64, EDGE), struct(2, 2, 64, EDGE), struct(2, 256, EDGE))
    return pl.pallas_call(
        functools.partial(item_kernel, stratum),
        out_shape=out + (struct(1024, 2 * EDGE, dtype=BF16),),
        in_specs=[SMEM] * 5 + [VMEM] * 8,
        out_specs=(VMEM,) * (len(out) + 1),
        scratch_shapes=scratch,
        compiler_params=PARAMS,
        cost_estimate=cost(12),
        name=f"item_step{stratum}",
    )(*scalars, *users[1:], state, *pieces)


def user_kernel(
    stratum,
    rank,
    count,
    user,
    item,
    counts,
    uf,
    uth,
    utl,
    v,
    vp,
    vs,
    errors,
    own,
    pair,
    sib,
    *rest,
):
    *outs, sums = rest
    mine = rank[0]
    for k in (1, 2, 3):
        sums[k] = jnp.zeros((1024, EDGE), F32)
    for p in range(SLOTS):
        slot = stratum * SLOTS + p
        which = item[0, slot] ^ mine

        @pl.when((p < count[0, stratum]) & (which != 0))
        def _():
            place = p if stratum == 0 else slot - SLOTS
            target = sums.at[which]
            add_tile(mine, place, (own, pair, sib), user[0, slot] * EDGE, target)

    last = stratum == STRATA - 1
    others = jnp.concatenate([vp[...], vs[0], vs[1]], axis=1)
    oh, ol = split(others)
    if last:
        rows = pl.ds(pl.multiple_of(mine * 64, 64), 64)
        kept = jnp.concatenate([v[rows, :], vp[rows, :], vs[0, rows, :], vs[1, rows, :]], axis=1)
        kh, kl = split(kept)
    else:
        rows = slice(None)
        vh, vl = split(v[...])
        kh = jnp.concatenate([vh, oh], axis=1)
        kl = jnp.concatenate([vl, ol], axis=1)
    for first in range(0, 1024, CHUNK):
        span = slice(first, first + CHUNK)
        predicted = three(dot, (uth[span, :], utl[span, :]), (oh, ol))
        lines = []
        for k in range(CHUNK // EDGE):
            top = first + k * EDGE
            line = []
            for j, other in enumerate((2, 1, 3)):
                live = counts[stratum, top // EDGE * 4 + (mine ^ other)]
                part = predicted[k * EDGE : (k + 1) * EDGE, j * EDGE : (j + 1) * EDGE]
                line.append(sums[other, top : top + EDGE, :] - live * part)
            lines.append(jnp.concatenate(line, axis=1))
        eh, el = split(jnp.concatenate(lines, axis=0))
        eh = jnp.concatenate([errors[span, :EDGE], eh], axis=1)
        el = jnp.concatenate([errors[span, EDGE:], el], axis=1)
        grad = three(dot_nt, (kh, kl), (eh, el))
        old = uf[rows, span]
        new = old + LR_USER * (grad - DECAY * old)
        if last:
            outs[0][:, span] = new
        else:
            store_users(new, first, first + CHUNK, *outs)


def user_step(stratum, scalars, users, v, others, errors, pieces):
    last = stratum == STRATA - 1
    return pl.pallas_call(
        functools.partial(user_kernel, stratum),
        out_shape=(struct(64, 1024),) if last else USER_SHAPES,
        in_specs=[SMEM] * 5 + [VMEM] * 10,
        out_specs=(VMEM,) * (1 if last else 5),
        scratch_shapes=[pltpu.VMEM((4, 1024, EDGE), F32)],
        compiler_params=PARAMS,
        cost_estimate=cost(20),
        name=f"user_step{stratum}",
    )(*scalars, users[0], users[3], users[4], v, *others, errors, *pieces)


def place_kernel(rank, near, far, items, accum):
    mine = rank[0]
    for part, first in ((near, 0), (far, 2)):
        for j in range(2):
            block = mine ^ (first ^ j)
            cols = pl.ds(pl.multiple_of(block * EDGE, EDGE), EDGE)
            items[:, cols] = part[j, 0]
            accum[:, cols] = part[j, 1]


def place_state(rank, near, far):
    return pl.pallas_call(
        place_kernel,
        out_shape=(struct(64, 512), struct(64, 512)),
        in_specs=[SMEM, VMEM, VMEM],
        out_specs=(VMEM, VMEM),
        compiler_params=PARAMS,
        cost_estimate=cost(2),
        name="place_state",
    )(rank, near, far)


def exchange(x, by):
    return lax.ppermute(x, "rank", [(r, r ^ by) for r in range(4)])


def send_on(x, by):
    n = lax.axis_size("blk")
    return lax.ppermute(
        x,
        ("blk", "rank"),
        [(o * 4 + r, (o + 1) % n * 4 + (r ^ by)) for o in range(n) for r in range(4)],
    )


def body(
    ratings,
    send_list,
    plan,
    block_count,
    block_user,
    block_item,
    user_factors,
    item_factors,
    item_accum,
):
    rank = lax.axis_index("rank").astype(jnp.int32).reshape(1)
    quarter = (user_factors, item_factors, item_accum)
    pair = exchange(jnp.concatenate(quarter, axis=1), 2)

    outgoing, counts = gather_outgoing(
        rank, send_list, block_count, block_user, block_item, ratings
    )
    received = lax.all_to_all(outgoing, "blk", split_axis=0, concat_axis=0, tiled=True)
    scalars = (rank, block_count, block_user, block_item, counts)

    first, rest = order_received(plan, received)
    first_pair = exchange(first, 2)

    pair, first = lax.optimization_barrier((pair, first))
    sib = exchange(pack(rank, *quarter, pair), 1)
    *users, state = prepare(rank, *quarter, pair, sib)

    rest, first_pair = lax.optimization_barrier((rest, first_pair))
    rest_pair = exchange(rest, 2)
    pieces = (first, first_pair, exchange(jnp.stack([first, first_pair]), 1))
    for stratum in range(STRATA):
        *out, errors = item_step(stratum, scalars, users, state, pieces)
        v = state[0]
        vp = exchange(v, 2)
        vp, errors = lax.optimization_barrier((vp, errors))
        vs = exchange(jnp.stack([v, vp]), 1)
        if stratum < STRATA - 1:
            state = send_on(out[0], 0)
        else:
            kept, passed = out[0], out[1]
            got = exchange(passed, 1)
            near = send_on(jnp.stack([kept[0], got[0]]), 0)
            far = send_on(jnp.stack([kept[1], got[1]]), 2)
        if stratum == 0:
            rest_pair, errors = lax.optimization_barrier((rest_pair, errors))
            rest_sib = exchange(jnp.stack([rest, rest_pair]), 1)
        users = user_step(stratum, scalars, users, v, (vp, vs), errors, pieces)
        users = list(users)
        if stratum == 0:
            pieces = (rest, rest_pair, rest_sib)
        if stratum < STRATA - 1:
            state, users, pieces = lax.optimization_barrier((state, users, pieces))
    near, far, users_out = lax.optimization_barrier((near, far, users[0]))
    items_out, accum_out = place_state(rank, near, far)
    return users_out, items_out, accum_out


def solution(mesh):
    placed = (
        P("blk", None, None),
        P("blk", None),
        P("blk", None),
        P("blk", None),
        P("blk", None),
        P("blk", None),
        P("rank", "blk"),
        P("rank", "blk"),
        P("rank", "blk"),
    )
    return jax.shard_map(
        body,
        mesh=mesh,
        in_specs=placed,
        out_specs=(P("rank", "blk"), P("rank", "blk"), P("rank", "blk")),
        check_vma=False,
    )
```

```python
import functools

import jax
import jax.numpy as jnp
from jax import lax
from jax.experimental import pallas as pl
from jax.experimental.pallas import tpu as pltpu
from jax.sharding import PartitionSpec as P

LR_USER = 0.01
LR_ITEM = 0.05
DECAY = 0.05
F32 = jnp.float32
BF16 = jnp.bfloat16
EDGE = 128
SLOTS = 16
STRATA = 4
QUARTER = 32
CHUNK = 256
VMEM = pl.BlockSpec(memory_space=pltpu.VMEM)
SMEM = pl.BlockSpec(memory_space=pltpu.SMEM)
HBM = pl.BlockSpec(memory_space=pltpu.HBM)
PARAMS = pltpu.CompilerParams(vmem_limit_bytes=16 * 2**20)


def cost(time):
    return pl.CostEstimate(flops=10**9 * time, bytes_accessed=3 * 10**6 * time, transcendentals=0)


def split(x):
    high = x.astype(BF16)
    return high, (x - high.astype(F32)).astype(BF16)


def dot(a, b):
    return jnp.dot(a, b, preferred_element_type=F32)


def dot_nt(a, b):
    return lax.dot_general(a, b, (((1,), (1,)), ((), ())), preferred_element_type=F32)


def three(product, a, b):
    return product(a[0], b[0]) + product(a[0], b[1]) + product(a[1], b[0])


def struct(*shape, dtype=F32):
    return jax.ShapeDtypeStruct(shape, dtype)


def gather_kernel(rank, routes, ratings, out, places, sems):
    fetch = pltpu.make_async_copy(routes, places, sems.at[0])
    fetch.start()
    fetch.wait()
    row = pl.multiple_of(rank[0] * QUARTER, QUARTER)
    for d in range(64):
        pltpu.make_async_copy(
            ratings.at[places[0, d], pl.ds(row, QUARTER), :], out.at[d], sems.at[1]
        ).start()
    pltpu.make_async_copy(out, out, sems.at[1]).wait()


def gather_outgoing(rank, routes, ratings):
    return pl.pallas_call(
        gather_kernel,
        out_shape=struct(64, QUARTER, EDGE, dtype=BF16),
        in_specs=[SMEM, HBM, HBM],
        out_specs=VMEM,
        scratch_shapes=[pltpu.SMEM((1, 64), jnp.int32), pltpu.SemaphoreType.DMA((2,))],
        compiler_params=pltpu.CompilerParams(vmem_limit_bytes=65 * 10**6),
        cost_estimate=cost(2),
        name="gather_outgoing",
    )(rank, routes, ratings)


def order_kernel(plan, received, *outs):
    for stratum, out in enumerate(outs):
        for p in range(SLOTS):
            out[p] = received[plan[0, stratum * SLOTS + p]]


def order_received(plan, received):
    return pl.pallas_call(
        order_kernel,
        out_shape=(struct(SLOTS, QUARTER, EDGE, dtype=BF16),) * STRATA,
        in_specs=[SMEM, VMEM],
        out_specs=(VMEM,) * STRATA,
        compiler_params=PARAMS,
        cost_estimate=cost(4),
        name="order_received",
    )(plan, received)


def block_of(ref, block):
    return ref[:, pl.ds(pl.multiple_of(block * EDGE, EDGE), EDGE)]


def store_users(uf, first, last, uf_ref, uh, ul, uth, utl):
    cols = slice(first, last)
    high, low = split(uf)
    uf_ref[:, cols] = uf
    uh[:, cols] = high
    ul[:, cols] = low
    turned = uf.T
    high, low = split(turned)
    uth[cols, :] = high
    utl[cols, :] = low


def group_rows(rank):
    return [pl.ds(pl.multiple_of((rank ^ k) * 64, 64), 64) for k in (0, 2, 1, 3)]


def offer_kernel(rank, count, user, item, users, items, accum, out, counts):
    for s in range(STRATA):
        for k in range(32):
            counts[s, k] = 0.0
        for p in range(SLOTS):
            slot = s * SLOTS + p
            where = user[0, slot] * 4 + item[0, slot]
            counts[s, where] += jnp.where(p < count[0, s], 1.0, 0.0)
    out[:, :1024] = users[...]
    for k, source in enumerate((items, accum)):
        for j in range(2):
            start = 1024 + (2 * k + j) * EDGE
            out[:, start : start + EDGE] = block_of(source, rank[0] ^ 2 ^ j)


def offer(rank, count, user, item, users, items, accum):
    return pl.pallas_call(
        offer_kernel,
        out_shape=(struct(64, 1536), struct(STRATA, 32)),
        in_specs=[SMEM] * 4 + [VMEM] * 3,
        out_specs=(VMEM, SMEM),
        compiler_params=PARAMS,
        cost_estimate=cost(2),
        name="offer",
    )(rank, count, user, item, users, items, accum)


def pack_kernel(rank, users, items, accum, pair, out):
    sibling = rank[0] ^ 1
    out[0, :, :1024] = users[...]
    out[1, :, :1024] = pair[:, :1024]
    for k, source in enumerate((items, accum)):
        cols = slice(1024 + k * EDGE, 1024 + (k + 1) * EDGE)
        out[0, :, cols] = block_of(source, sibling)
        start = 1024 + (2 * k + 1) * EDGE
        out[1, :, cols] = pair[:, start : start + EDGE]


def pack(rank, users, items, accum, pair):
    return pl.pallas_call(
        pack_kernel,
        out_shape=struct(2, 64, 1280),
        in_specs=[SMEM] + [VMEM] * 4,
        out_specs=VMEM,
        compiler_params=PARAMS,
        cost_estimate=cost(0),
        name="pack",
    )(rank, users, items, accum, pair)


def prepare_kernel(
    rank, own, items, accum, pair, sib, uf, uh, ul, uth, utl, state, users
):
    mine = rank[0]
    places = group_rows(mine)
    parts = (own, pair.at[:, :1024], sib.at[0, :, :1024], sib.at[1, :, :1024])
    for place, part in zip(places, parts):
        users[place, :] = part[...]
    for first in range(0, 1024, CHUNK):
        last = first + CHUNK
        store_users(users[:, first:last], first, last, uf, uh, ul, uth, utl)
    for k, own_part in enumerate((items, accum)):
        state[k, places[0], :] = block_of(own_part, mine)
        start = 1024 + 2 * k * EDGE
        state[k, places[1], :] = pair[:, start : start + EDGE]
        for j in range(2):
            start = 1024 + EDGE * k
            state[k, places[2 + j], :] = sib[j, :, start : start + EDGE]


USER_SHAPES = (
    struct(256, 1024),
    struct(256, 1024, dtype=BF16),
    struct(256, 1024, dtype=BF16),
    struct(1024, 256, dtype=BF16),
    struct(1024, 256, dtype=BF16),
)


def prepare(rank, own, items, accum, pair, sib):
    return pl.pallas_call(
        prepare_kernel,
        out_shape=USER_SHAPES + (struct(2, 256, EDGE),),
        in_specs=[SMEM] + [VMEM] * 5,
        out_specs=(VMEM,) * 6,
        scratch_shapes=[pltpu.VMEM((256, 1024), F32)],
        compiler_params=PARAMS,
        cost_estimate=cost(0),
        name="prepare",
    )(rank, own, items, accum, pair, sib)


def add_tile(rank, place, pieces, top, sums):
    for k, piece in zip((0, 2, 1, 3), pieces):
        start = pl.multiple_of(top + (rank ^ k) * QUARTER, QUARTER)
        sums[pl.ds(start, QUARTER), :] += piece[place].astype(F32)


def item_kernel(
    stratum, rank, count, user, item, counts, uh, ul, uth, utl, state, *rest
):
    pieces, (*outs, errors, sums) = rest[:4], rest[4:]
    mine = rank[0]
    sums[...] = jnp.zeros_like(sums)
    for p in range(SLOTS):
        slot = stratum * SLOTS + p

        @pl.when((p < count[0, stratum]) & (item[0, slot] == mine))
        def _():
            add_tile(mine, p, pieces, user[0, slot] * EDGE, sums)

    items = state[0]
    vh, vl = split(items)
    both = jnp.concatenate([vh, vl], axis=1)
    grad = jnp.zeros_like(items)
    for first in range(0, 1024, CHUNK):
        rows = slice(first, first + CHUNK)
        wide = dot(uth[rows, :], both)
        predicted = wide[:, :EDGE] + wide[:, EDGE:] + dot(utl[rows, :], vh)
        parts = []
        for k in range(CHUNK // EDGE):
            top = first + k * EDGE
            live = counts[stratum, top // EDGE * 4 + mine]
            parts.append(sums[top : top + EDGE, :] - live * predicted[k * EDGE : (k + 1) * EDGE])
        eh, el = split(jnp.concatenate(parts, axis=0))
        es = jnp.concatenate([eh, el], axis=1)
        errors[rows, :] = es
        wide = dot(uh[:, rows], es)
        grad += wide[:, :EDGE] + wide[:, EDGE:] + dot(ul[:, rows], eh)
    grad = grad - DECAY * items
    accum = state[1] + grad * grad
    items = items + LR_ITEM * grad / jnp.sqrt(accum)
    if stratum < STRATA - 1:
        outs[0][0] = items
        outs[0][1] = accum
    else:
        kept, passed, spot = outs[0], outs[1], outs[2]
        spot[0] = items
        spot[1] = accum
        for j, rows in enumerate(group_rows(mine)):
            target = kept if j < 2 else passed
            for k in range(2):
                target[j % 2, k] = spot[k, rows, :]


def item_step(stratum, scalars, users, state, pieces):
    scratch = [pltpu.VMEM((1024, EDGE), F32)]
    if stratum < STRATA - 1:
        out = (struct(2, 256, EDGE),)
    else:
        out = (struct(2, 2, 64, EDGE), struct(2, 2, 64, EDGE), struct(2, 256, EDGE))
    return pl.pallas_call(
        functools.partial(item_kernel, stratum),
        out_shape=out + (struct(1024, 2 * EDGE, dtype=BF16),),
        in_specs=[SMEM] * 5 + [VMEM] * 9,
        out_specs=(VMEM,) * (len(out) + 1),
        scratch_shapes=scratch,
        compiler_params=PARAMS,
        cost_estimate=cost(12),
        name=f"item_step{stratum}",
    )(*scalars, *users[1:], state, *pieces)


def user_kernel(
    stratum,
    rank,
    count,
    user,
    item,
    counts,
    uf,
    uth,
    utl,
    v,
    vp,
    vs,
    vd,
    errors,
    *rest,
):
    pieces, (*outs, sums) = rest[:4], rest[4:]
    mine = rank[0]
    for k in (1, 2, 3):
        sums[k] = jnp.zeros((1024, EDGE), F32)
    for p in range(SLOTS):
        slot = stratum * SLOTS + p
        which = item[0, slot] ^ mine

        @pl.when((p < count[0, stratum]) & (which != 0))
        def _():
            target = sums.at[which]
            add_tile(mine, p, pieces, user[0, slot] * EDGE, target)

    last = stratum == STRATA - 1
    others = jnp.concatenate([vp[...], vs[...], vd[...]], axis=1)
    oh, ol = split(others)
    if last:
        rows = pl.ds(pl.multiple_of(mine * 64, 64), 64)
        kept = jnp.concatenate([x[rows, :] for x in (v, vp, vs, vd)], axis=1)
        kh, kl = split(kept)
    else:
        rows = slice(None)
        vh, vl = split(v[...])
        kh = jnp.concatenate([vh, oh], axis=1)
        kl = jnp.concatenate([vl, ol], axis=1)
    for first in range(0, 1024, CHUNK):
        span = slice(first, first + CHUNK)
        predicted = three(dot, (uth[span, :], utl[span, :]), (oh, ol))
        lines = []
        for k in range(CHUNK // EDGE):
            top = first + k * EDGE
            line = []
            for j, other in enumerate((2, 1, 3)):
                live = counts[stratum, top // EDGE * 4 + (mine ^ other)]
                part = predicted[k * EDGE : (k + 1) * EDGE, j * EDGE : (j + 1) * EDGE]
                line.append(sums[other, top : top + EDGE, :] - live * part)
            lines.append(jnp.concatenate(line, axis=1))
        eh, el = split(jnp.concatenate(lines, axis=0))
        eh = jnp.concatenate([errors[span, :EDGE], eh], axis=1)
        el = jnp.concatenate([errors[span, EDGE:], el], axis=1)
        grad = three(dot_nt, (kh, kl), (eh, el))
        old = uf[rows, span]
        new = old + LR_USER * (grad - DECAY * old)
        if last:
            outs[0][:, span] = new
        else:
            store_users(new, first, first + CHUNK, *outs)


def user_step(stratum, scalars, users, v, others, errors, pieces):
    last = stratum == STRATA - 1
    return pl.pallas_call(
        functools.partial(user_kernel, stratum),
        out_shape=(struct(64, 1024),) if last else USER_SHAPES,
        in_specs=[SMEM] * 5 + [VMEM] * 12,
        out_specs=(VMEM,) * (1 if last else 5),
        scratch_shapes=[pltpu.VMEM((4, 1024, EDGE), F32)],
        compiler_params=PARAMS,
        cost_estimate=cost(0),
        name=f"user_step{stratum}",
    )(*scalars, users[0], users[3], users[4], v, *others, errors, *pieces)


def place_kernel(rank, near, far, items, accum):
    mine = rank[0]
    for part, first in ((near, 0), (far, 2)):
        for j in range(2):
            block = mine ^ (first ^ j)
            cols = pl.ds(pl.multiple_of(block * EDGE, EDGE), EDGE)
            items[:, cols] = part[j, 0]
            accum[:, cols] = part[j, 1]


def place_state(rank, near, far):
    return pl.pallas_call(
        place_kernel,
        out_shape=(struct(64, 512), struct(64, 512)),
        in_specs=[SMEM, VMEM, VMEM],
        out_specs=(VMEM, VMEM),
        compiler_params=PARAMS,
        cost_estimate=cost(2),
        name="place_state",
    )(rank, near, far)


def exchange(x, by):
    return lax.ppermute(x, "rank", [(r, r ^ by) for r in range(4)])


def send_on(x, by):
    n = lax.axis_size("blk")
    return lax.ppermute(
        x,
        ("blk", "rank"),
        [(o * 4 + r, (o + 1) % n * 4 + (r ^ by)) for o in range(n) for r in range(4)],
    )


def body(
    ratings,
    send_list,
    plan,
    block_count,
    block_user,
    block_item,
    user_factors,
    item_factors,
    item_accum,
):
    rank = lax.axis_index("rank").astype(jnp.int32).reshape(1)
    quarter = (user_factors, item_factors, item_accum)
    offered, counts = offer(rank, block_count, block_user, block_item, *quarter)
    pair = exchange(offered, 2)
    scalars = (rank, block_count, block_user, block_item, counts)

    outgoing = gather_outgoing(rank, send_list, ratings)
    received = lax.all_to_all(outgoing, "blk", split_axis=0, concat_axis=0, tiled=True)

    tiles = list(order_received(plan, received))
    first = tiles[0]
    first_pair = exchange(first, 2)
    first_sib = exchange(first, 1)

    pair, first_sib = lax.optimization_barrier((pair, first_sib))
    sib = exchange(pack(rank, *quarter, pair), 1)
    *users, state = prepare(rank, *quarter, pair, sib)

    tiles[1], first_pair = lax.optimization_barrier((tiles[1], first_pair))
    next_pair = exchange(tiles[1], 2)
    pieces = (first, first_pair, first_sib, exchange(first_pair, 1))
    for stratum in range(STRATA):
        last = stratum == STRATA - 1
        *out, errors = item_step(stratum, scalars, users, state, pieces)
        v = state[0]
        vp = exchange(v, 2)
        if last:
            kept, passed = out[0], out[1]
            got = exchange(passed, 1)
            near = send_on(jnp.stack([kept[0], got[0]]), 0)
            far = send_on(jnp.stack([kept[1], got[1]]), 2)
            late, errors = lax.optimization_barrier((v, errors))
        else:
            state = send_on(out[0], 0)
            late, own, errors = lax.optimization_barrier((v, tiles[stratum + 1], errors))
            next_sib = exchange(own, 1)
            next_pair, errors = lax.optimization_barrier((next_pair, errors))
            next_diag = exchange(next_pair, 1)
        vs = exchange(late, 1)
        vp, errors = lax.optimization_barrier((vp, errors))
        vd = exchange(vp, 1)
        if not last:
            after = (tiles[stratum + 1], next_pair, next_sib, next_diag)
            if stratum < 2:
                tiles[stratum + 2], vd = lax.optimization_barrier((tiles[stratum + 2], vd))
                next_pair = exchange(tiles[stratum + 2], 2)
            vs, vd, after, errors = lax.optimization_barrier((vs, vd, after, errors))
        users = user_step(stratum, scalars, users, v, (vp, vs, vd), errors, pieces)
        if not last:
            pieces = after
            state, users, pieces = lax.optimization_barrier((state, users, pieces))
    near, far, users_out = lax.optimization_barrier((near, far, users[0]))
    items_out, accum_out = place_state(rank, near, far)
    return users_out, items_out, accum_out


def solution(mesh):
    placed = (
        P("blk", None, None),
        P("blk", None),
        P("blk", None),
        P("blk", None),
        P("blk", None),
        P("blk", None),
        P("rank", "blk"),
        P("rank", "blk"),
        P("rank", "blk"),
    )
    return jax.shard_map(
        body,
        mesh=mesh,
        in_specs=placed,
        out_specs=(P("rank", "blk"), P("rank", "blk"), P("rank", "blk")),
        check_vma=False,
    )
```

```python
import functools

import jax
import jax.numpy as jnp
from jax import lax
from jax.experimental import pallas as pl
from jax.experimental.pallas import tpu as pltpu
from jax.sharding import PartitionSpec as P

LR_USER = 0.01
LR_ITEM = 0.05
DECAY = 0.05
F32 = jnp.float32
BF16 = jnp.bfloat16
EDGE = 128
SLOTS = 16
STRATA = 4
QUARTER = 32
CHUNK = 256
VMEM = pl.BlockSpec(memory_space=pltpu.VMEM)
SMEM = pl.BlockSpec(memory_space=pltpu.SMEM)
HBM = pl.BlockSpec(memory_space=pltpu.HBM)
PARAMS = pltpu.CompilerParams(vmem_limit_bytes=16 * 2**20)


def cost(time):
    return pl.CostEstimate(flops=10**9 * time, bytes_accessed=3 * 10**6 * time, transcendentals=0)


def split(x):
    high = x.astype(BF16)
    return high, (x - high.astype(F32)).astype(BF16)


def dot(a, b):
    return jnp.dot(a, b, preferred_element_type=F32)


def dot_nt(a, b):
    return lax.dot_general(a, b, (((1,), (1,)), ((), ())), preferred_element_type=F32)


def three(product, a, b):
    return product(a[0], b[0]) + product(a[0], b[1]) + product(a[1], b[0])


def struct(*shape, dtype=F32):
    return jax.ShapeDtypeStruct(shape, dtype)


def gather_kernel(rank, routes, ratings, out, places, sems):
    fetch = pltpu.make_async_copy(routes, places, sems.at[0])
    fetch.start()
    fetch.wait()
    row = pl.multiple_of(rank[0] * QUARTER, QUARTER)
    for d in range(64):
        pltpu.make_async_copy(
            ratings.at[places[0, d], pl.ds(row, QUARTER), :], out.at[d], sems.at[1]
        ).start()
    pltpu.make_async_copy(out, out, sems.at[1]).wait()


def gather_outgoing(rank, routes, ratings):
    return pl.pallas_call(
        gather_kernel,
        out_shape=struct(64, QUARTER, EDGE, dtype=BF16),
        in_specs=[SMEM, HBM, HBM],
        out_specs=VMEM,
        scratch_shapes=[pltpu.SMEM((1, 64), jnp.int32), pltpu.SemaphoreType.DMA((2,))],
        compiler_params=pltpu.CompilerParams(vmem_limit_bytes=65 * 10**6),
        cost_estimate=cost(2),
        name="gather_outgoing",
    )(rank, routes, ratings)


def order_kernel(plan, received, *outs):
    for stratum, out in enumerate(outs):
        for p in range(SLOTS):
            out[p] = received[plan[0, stratum * SLOTS + p]]


def order_received(plan, received):
    return pl.pallas_call(
        order_kernel,
        out_shape=(struct(SLOTS, QUARTER, EDGE, dtype=BF16),) * STRATA,
        in_specs=[SMEM, VMEM],
        out_specs=(VMEM,) * STRATA,
        compiler_params=PARAMS,
        cost_estimate=cost(4),
        name="order_received",
    )(plan, received)


def block_of(ref, block):
    return ref[:, pl.ds(pl.multiple_of(block * EDGE, EDGE), EDGE)]


def store_users(uf, first, last, uf_ref, uh, ul, uth, utl):
    cols = slice(first, last)
    high, low = split(uf)
    uf_ref[:, cols] = uf
    uh[:, cols] = high
    ul[:, cols] = low
    turned = uf.T
    high, low = split(turned)
    uth[cols, :] = high
    utl[cols, :] = low


def group_rows(rank):
    return [pl.ds(pl.multiple_of((rank ^ k) * 64, 64), 64) for k in (0, 2, 1, 3)]


def offer_kernel(rank, count, user, item, users, items, accum, out, counts):
    for s in range(STRATA):
        for k in range(32):
            counts[s, k] = 0.0
        for p in range(SLOTS):
            slot = s * SLOTS + p
            where = user[0, slot] * 4 + item[0, slot]
            counts[s, where] += jnp.where(p < count[0, s], 1.0, 0.0)
    out[:, :1024] = users[...]
    for k, source in enumerate((items, accum)):
        for j in range(2):
            start = 1024 + (2 * k + j) * EDGE
            out[:, start : start + EDGE] = block_of(source, rank[0] ^ 2 ^ j)


def offer(rank, count, user, item, users, items, accum):
    return pl.pallas_call(
        offer_kernel,
        out_shape=(struct(64, 1536), struct(STRATA, 32)),
        in_specs=[SMEM] * 4 + [VMEM] * 3,
        out_specs=(VMEM, SMEM),
        compiler_params=PARAMS,
        cost_estimate=cost(2),
        name="offer",
    )(rank, count, user, item, users, items, accum)


def pack_kernel(rank, users, items, accum, pair, out):
    sibling = rank[0] ^ 1
    out[0, :, :1024] = users[...]
    out[1, :, :1024] = pair[:, :1024]
    for k, source in enumerate((items, accum)):
        cols = slice(1024 + k * EDGE, 1024 + (k + 1) * EDGE)
        out[0, :, cols] = block_of(source, sibling)
        start = 1024 + (2 * k + 1) * EDGE
        out[1, :, cols] = pair[:, start : start + EDGE]


def pack(rank, users, items, accum, pair):
    return pl.pallas_call(
        pack_kernel,
        out_shape=struct(2, 64, 1280),
        in_specs=[SMEM] + [VMEM] * 4,
        out_specs=VMEM,
        compiler_params=PARAMS,
        cost_estimate=cost(0),
        name="pack",
    )(rank, users, items, accum, pair)


def prepare_kernel(
    rank, own, items, accum, pair, sib, uf, uh, ul, uth, utl, state, users
):
    mine = rank[0]
    places = group_rows(mine)
    parts = (own, pair.at[:, :1024], sib.at[0, :, :1024], sib.at[1, :, :1024])
    for place, part in zip(places, parts):
        users[place, :] = part[...]
    for first in range(0, 1024, CHUNK):
        last = first + CHUNK
        store_users(users[:, first:last], first, last, uf, uh, ul, uth, utl)
    for k, own_part in enumerate((items, accum)):
        state[k, places[0], :] = block_of(own_part, mine)
        start = 1024 + 2 * k * EDGE
        state[k, places[1], :] = pair[:, start : start + EDGE]
        for j in range(2):
            start = 1024 + EDGE * k
            state[k, places[2 + j], :] = sib[j, :, start : start + EDGE]


USER_SHAPES = (
    struct(256, 1024),
    struct(256, 1024, dtype=BF16),
    struct(256, 1024, dtype=BF16),
    struct(1024, 256, dtype=BF16),
    struct(1024, 256, dtype=BF16),
)


def prepare(rank, own, items, accum, pair, sib):
    return pl.pallas_call(
        prepare_kernel,
        out_shape=USER_SHAPES + (struct(2, 256, EDGE),),
        in_specs=[SMEM] + [VMEM] * 5,
        out_specs=(VMEM,) * 6,
        scratch_shapes=[pltpu.VMEM((256, 1024), F32)],
        compiler_params=PARAMS,
        cost_estimate=cost(0),
        name="prepare",
    )(rank, own, items, accum, pair, sib)


def add_tile(rank, place, pieces, top, sums):
    for k, piece in zip((0, 2, 1, 3), pieces):
        start = pl.multiple_of(top + (rank ^ k) * QUARTER, QUARTER)
        sums[pl.ds(start, QUARTER), :] += piece[place].astype(F32)


def sum_kernel(stratum, rank, count, user, item, *rest):
    pieces, sums = rest[:4], rest[4]
    mine = rank[0]
    sums[...] = jnp.zeros_like(sums)
    for p in range(SLOTS):
        slot = stratum * SLOTS + p

        @pl.when(p < count[0, stratum])
        def _():
            target = sums.at[item[0, slot] ^ mine]
            add_tile(mine, p, pieces, user[0, slot] * EDGE, target)


def sum_tiles(stratum, scalars, pieces):
    return pl.pallas_call(
        functools.partial(sum_kernel, stratum),
        out_shape=struct(4, 1024, EDGE),
        in_specs=[SMEM] * 4 + [VMEM] * 4,
        out_specs=VMEM,
        compiler_params=PARAMS,
        cost_estimate=cost(30 if stratum == 0 else 0),
        name=f"sum_tiles{stratum}",
    )(*scalars[:4], *pieces)


def item_kernel(stratum, rank, counts, uh, ul, uth, utl, state, sums, *rest):
    *outs, errors = rest
    mine = rank[0]
    items = state[0]
    vh, vl = split(items)
    both = jnp.concatenate([vh, vl], axis=1)
    grad = jnp.zeros_like(items)
    for first in range(0, 1024, CHUNK):
        rows = slice(first, first + CHUNK)
        wide = dot(uth[rows, :], both)
        predicted = wide[:, :EDGE] + wide[:, EDGE:] + dot(utl[rows, :], vh)
        parts = []
        for k in range(CHUNK // EDGE):
            top = first + k * EDGE
            live = counts[stratum, top // EDGE * 4 + mine]
            parts.append(sums[0, top : top + EDGE, :] - live * predicted[k * EDGE : (k + 1) * EDGE])
        eh, el = split(jnp.concatenate(parts, axis=0))
        es = jnp.concatenate([eh, el], axis=1)
        errors[rows, :] = es
        wide = dot(uh[:, rows], es)
        grad += wide[:, :EDGE] + wide[:, EDGE:] + dot(ul[:, rows], eh)
    grad = grad - DECAY * items
    accum = state[1] + grad * grad
    items = items + LR_ITEM * grad / jnp.sqrt(accum)
    if stratum < STRATA - 1:
        outs[0][0] = items
        outs[0][1] = accum
    else:
        kept, passed, spot = outs[0], outs[1], outs[2]
        spot[0] = items
        spot[1] = accum
        for j, rows in enumerate(group_rows(mine)):
            target = kept if j < 2 else passed
            for k in range(2):
                target[j % 2, k] = spot[k, rows, :]


def item_step(stratum, scalars, users, state, sums):
    if stratum < STRATA - 1:
        out = (struct(2, 256, EDGE),)
    else:
        out = (struct(2, 2, 64, EDGE), struct(2, 2, 64, EDGE), struct(2, 256, EDGE))
    return pl.pallas_call(
        functools.partial(item_kernel, stratum),
        out_shape=out + (struct(1024, 2 * EDGE, dtype=BF16),),
        in_specs=[SMEM] * 2 + [VMEM] * 6,
        out_specs=(VMEM,) * (len(out) + 1),
        compiler_params=PARAMS,
        cost_estimate=cost(12),
        name=f"item_step{stratum}",
    )(scalars[0], scalars[4], *users[1:], state, sums)


def user_kernel(stratum, rank, counts, uf, uth, utl, v, vp, vs, vd, errors, sums, *outs):
    mine = rank[0]
    last = stratum == STRATA - 1
    others = jnp.concatenate([vp[...], vs[...], vd[...]], axis=1)
    oh, ol = split(others)
    if last:
        rows = pl.ds(pl.multiple_of(mine * 64, 64), 64)
        kept = jnp.concatenate([x[rows, :] for x in (v, vp, vs, vd)], axis=1)
        kh, kl = split(kept)
    else:
        rows = slice(None)
        vh, vl = split(v[...])
        kh = jnp.concatenate([vh, oh], axis=1)
        kl = jnp.concatenate([vl, ol], axis=1)
    for first in range(0, 1024, CHUNK):
        span = slice(first, first + CHUNK)
        predicted = three(dot, (uth[span, :], utl[span, :]), (oh, ol))
        lines = []
        for k in range(CHUNK // EDGE):
            top = first + k * EDGE
            line = []
            for j, other in enumerate((2, 1, 3)):
                live = counts[stratum, top // EDGE * 4 + (mine ^ other)]
                part = predicted[k * EDGE : (k + 1) * EDGE, j * EDGE : (j + 1) * EDGE]
                line.append(sums[other, top : top + EDGE, :] - live * part)
            lines.append(jnp.concatenate(line, axis=1))
        eh, el = split(jnp.concatenate(lines, axis=0))
        eh = jnp.concatenate([errors[span, :EDGE], eh], axis=1)
        el = jnp.concatenate([errors[span, EDGE:], el], axis=1)
        grad = three(dot_nt, (kh, kl), (eh, el))
        old = uf[rows, span]
        new = old + LR_USER * (grad - DECAY * old)
        if last:
            outs[0][:, span] = new
        else:
            store_users(new, first, first + CHUNK, *outs)


def user_step(stratum, scalars, users, v, others, errors, sums):
    last = stratum == STRATA - 1
    return pl.pallas_call(
        functools.partial(user_kernel, stratum),
        out_shape=(struct(64, 1024),) if last else USER_SHAPES,
        in_specs=[SMEM] * 2 + [VMEM] * 9,
        out_specs=(VMEM,) * (1 if last else 5),
        compiler_params=PARAMS,
        cost_estimate=cost(0),
        name=f"user_step{stratum}",
    )(scalars[0], scalars[4], users[0], users[3], users[4], v, *others, errors, sums)


def place_kernel(rank, near, far, items, accum):
    mine = rank[0]
    for part, first in ((near, 0), (far, 2)):
        for j in range(2):
            block = mine ^ (first ^ j)
            cols = pl.ds(pl.multiple_of(block * EDGE, EDGE), EDGE)
            items[:, cols] = part[j, 0]
            accum[:, cols] = part[j, 1]


def place_state(rank, near, far):
    return pl.pallas_call(
        place_kernel,
        out_shape=(struct(64, 512), struct(64, 512)),
        in_specs=[SMEM, VMEM, VMEM],
        out_specs=(VMEM, VMEM),
        compiler_params=PARAMS,
        cost_estimate=cost(2),
        name="place_state",
    )(rank, near, far)


def exchange(x, by):
    return lax.ppermute(x, "rank", [(r, r ^ by) for r in range(4)])


def send_on(x, by):
    n = lax.axis_size("blk")
    return lax.ppermute(
        x,
        ("blk", "rank"),
        [(o * 4 + r, (o + 1) % n * 4 + (r ^ by)) for o in range(n) for r in range(4)],
    )


def body(
    ratings,
    send_list,
    plan,
    block_count,
    block_user,
    block_item,
    user_factors,
    item_factors,
    item_accum,
):
    rank = lax.axis_index("rank").astype(jnp.int32).reshape(1)
    quarter = (user_factors, item_factors, item_accum)
    offered, counts = offer(rank, block_count, block_user, block_item, *quarter)
    pair = exchange(offered, 2)
    scalars = (rank, block_count, block_user, block_item, counts)

    outgoing = gather_outgoing(rank, send_list, ratings)
    received = lax.all_to_all(outgoing, "blk", split_axis=0, concat_axis=0, tiled=True)

    tiles = list(order_received(plan, received))
    first = tiles[0]
    first_pair = exchange(first, 2)
    first_sib = exchange(first, 1)

    pair, tiles[2] = lax.optimization_barrier((pair, tiles[2]))
    sib = exchange(pack(rank, *quarter, pair), 1)
    *users, state = prepare(rank, *quarter, pair, sib)

    tiles[1], first_pair = lax.optimization_barrier((tiles[1], first_pair))
    next_pair = exchange(tiles[1], 2)
    sums = sum_tiles(0, scalars, (first, first_pair, first_sib, exchange(first_pair, 1)))
    for stratum in range(STRATA):
        last = stratum == STRATA - 1
        *out, errors = item_step(stratum, scalars, users, state, sums)
        v = state[0]
        vp = exchange(v, 2)
        if last:
            kept, passed = out[0], out[1]
            got = exchange(passed, 1)
            near = send_on(jnp.stack([kept[0], got[0]]), 0)
            far = send_on(jnp.stack([kept[1], got[1]]), 2)
            late, got, errors = lax.optimization_barrier((v, got, errors))
        else:
            state = send_on(out[0], 0)
            late, own, errors = lax.optimization_barrier((v, tiles[stratum + 1], errors))
            next_sib = exchange(own, 1)
            next_pair, errors = lax.optimization_barrier((next_pair, errors))
            next_diag = exchange(next_pair, 1)
        vs = exchange(late, 1)
        vp, errors = lax.optimization_barrier((vp, errors))
        if last:
            vd = jnp.concatenate([exchange(vp[:128], 1), exchange(vp[128:], 1)])
        else:
            vd = exchange(vp, 1)
        if not last:
            after = (tiles[stratum + 1], next_pair, next_sib, next_diag)
            if stratum < 2:
                tiles[stratum + 2], vd = lax.optimization_barrier((tiles[stratum + 2], vd))
                next_pair = exchange(tiles[stratum + 2], 2)
            vs, vd, after, errors = lax.optimization_barrier((vs, vd, after, errors))
        users = user_step(stratum, scalars, users, v, (vp, vs, vd), errors, sums)
        if not last:
            sums = sum_tiles(stratum + 1, scalars, after)
            state, users, sums = lax.optimization_barrier((state, users, sums))
    near, far, users_out = lax.optimization_barrier((near, far, users[0]))
    items_out, accum_out = place_state(rank, near, far)
    return users_out, items_out, accum_out


def solution(mesh):
    placed = (
        P("blk", None, None),
        P("blk", None),
        P("blk", None),
        P("blk", None),
        P("blk", None),
        P("blk", None),
        P("rank", "blk"),
        P("rank", "blk"),
        P("rank", "blk"),
    )
    return jax.shard_map(
        body,
        mesh=mesh,
        in_specs=placed,
        out_specs=(P("rank", "blk"), P("rank", "blk"), P("rank", "blk")),
        check_vma=False,
    )
```

```python
import functools

import jax
import jax.numpy as jnp
from jax import lax
from jax.experimental import pallas as pl
from jax.experimental.pallas import tpu as pltpu
from jax.sharding import PartitionSpec as P

LR_USER = 0.01
LR_ITEM = 0.05
DECAY = 0.05
F32 = jnp.float32
BF16 = jnp.bfloat16
EDGE = 128
SLOTS = 16
STRATA = 4
QUARTER = 32
CHUNK = 1024
VMEM = pl.BlockSpec(memory_space=pltpu.VMEM)
SMEM = pl.BlockSpec(memory_space=pltpu.SMEM)
HBM = pl.BlockSpec(memory_space=pltpu.HBM)
PARAMS = pltpu.CompilerParams(vmem_limit_bytes=16 * 2**20)


def cost(time):
    return pl.CostEstimate(flops=10**9 * time, bytes_accessed=3 * 10**6 * time, transcendentals=0)


def split(x):
    high = x.astype(BF16)
    return high, (x - high.astype(F32)).astype(BF16)


def dot(a, b):
    return jnp.dot(a, b, preferred_element_type=F32)


def dot_nt(a, b):
    return lax.dot_general(a, b, (((1,), (1,)), ((), ())), preferred_element_type=F32)


def three(product, a, b):
    return product(a[0], b[0]) + product(a[0], b[1]) + product(a[1], b[0])


def struct(*shape, dtype=F32):
    return jax.ShapeDtypeStruct(shape, dtype)


def gather_kernel(rank, routes, ratings, out, places, sems):
    fetch = pltpu.make_async_copy(routes, places, sems.at[0])
    fetch.start()
    fetch.wait()
    row = pl.multiple_of(rank[0] * QUARTER, QUARTER)
    for d in range(64):
        pltpu.make_async_copy(
            ratings.at[places[0, d], pl.ds(row, QUARTER), :], out.at[d], sems.at[1]
        ).start()
    pltpu.make_async_copy(out, out, sems.at[1]).wait()


def gather_outgoing(rank, routes, ratings):
    return pl.pallas_call(
        gather_kernel,
        out_shape=struct(64, QUARTER, EDGE, dtype=BF16),
        in_specs=[SMEM, HBM, HBM],
        out_specs=VMEM,
        scratch_shapes=[pltpu.SMEM((1, 64), jnp.int32), pltpu.SemaphoreType.DMA((2,))],
        compiler_params=pltpu.CompilerParams(vmem_limit_bytes=65 * 10**6),
        cost_estimate=cost(2),
        name="gather_outgoing",
    )(rank, routes, ratings)


def order_kernel(plan, received, *outs):
    for stratum, out in enumerate(outs):
        for p in range(SLOTS):
            out[p] = received[plan[0, stratum * SLOTS + p]]


def order_received(plan, received):
    return pl.pallas_call(
        order_kernel,
        out_shape=(struct(SLOTS, QUARTER, EDGE, dtype=BF16),) * STRATA,
        in_specs=[SMEM, VMEM],
        out_specs=(VMEM,) * STRATA,
        compiler_params=PARAMS,
        cost_estimate=cost(4),
        name="order_received",
    )(plan, received)


def block_of(ref, block):
    return ref[:, pl.ds(pl.multiple_of(block * EDGE, EDGE), EDGE)]


def store_users(uf, first, last, uf_ref, uh, ul, uth, utl):
    cols = slice(first, last)
    high, low = split(uf)
    uf_ref[:, cols] = uf
    uh[:, cols] = high
    ul[:, cols] = low
    turned = uf.T
    high, low = split(turned)
    uth[cols, :] = high
    utl[cols, :] = low


def group_rows(rank):
    return [pl.ds(pl.multiple_of((rank ^ k) * 64, 64), 64) for k in (0, 2, 1, 3)]


def offer_kernel(rank, count, user, item, users, items, accum, out, counts):
    for s in range(STRATA):
        for k in range(32):
            counts[s, k] = 0.0
        for p in range(SLOTS):
            slot = s * SLOTS + p
            where = user[0, slot] * 4 + item[0, slot]
            counts[s, where] += jnp.where(p < count[0, s], 1.0, 0.0)
    out[:, :1024] = users[...]
    for k, source in enumerate((items, accum)):
        for j in range(2):
            start = 1024 + (2 * k + j) * EDGE
            out[:, start : start + EDGE] = block_of(source, rank[0] ^ 2 ^ j)


def offer(rank, count, user, item, users, items, accum):
    return pl.pallas_call(
        offer_kernel,
        out_shape=(struct(64, 1536), struct(STRATA, 32)),
        in_specs=[SMEM] * 4 + [VMEM] * 3,
        out_specs=(VMEM, SMEM),
        compiler_params=PARAMS,
        cost_estimate=cost(2),
        name="offer",
    )(rank, count, user, item, users, items, accum)


def pack_kernel(rank, users, items, accum, pair, out):
    sibling = rank[0] ^ 1
    out[0, :, :1024] = users[...]
    out[1, :, :1024] = pair[:, :1024]
    for k, source in enumerate((items, accum)):
        cols = slice(1024 + k * EDGE, 1024 + (k + 1) * EDGE)
        out[0, :, cols] = block_of(source, sibling)
        start = 1024 + (2 * k + 1) * EDGE
        out[1, :, cols] = pair[:, start : start + EDGE]


def pack(rank, users, items, accum, pair):
    return pl.pallas_call(
        pack_kernel,
        out_shape=struct(2, 64, 1280),
        in_specs=[SMEM] + [VMEM] * 4,
        out_specs=VMEM,
        compiler_params=PARAMS,
        cost_estimate=cost(0),
        name="pack",
    )(rank, users, items, accum, pair)


def prepare_kernel(
    rank, own, items, accum, pair, sib, uf, uh, ul, uth, utl, state, users
):
    mine = rank[0]
    places = group_rows(mine)
    parts = (own, pair.at[:, :1024], sib.at[0, :, :1024], sib.at[1, :, :1024])
    for place, part in zip(places, parts):
        users[place, :] = part[...]
    for first in range(0, 1024, CHUNK):
        last = first + CHUNK
        store_users(users[:, first:last], first, last, uf, uh, ul, uth, utl)
    for k, own_part in enumerate((items, accum)):
        state[k, places[0], :] = block_of(own_part, mine)
        start = 1024 + 2 * k * EDGE
        state[k, places[1], :] = pair[:, start : start + EDGE]
        for j in range(2):
            start = 1024 + EDGE * k
            state[k, places[2 + j], :] = sib[j, :, start : start + EDGE]


USER_SHAPES = (
    struct(256, 1024),
    struct(256, 1024, dtype=BF16),
    struct(256, 1024, dtype=BF16),
    struct(1024, 256, dtype=BF16),
    struct(1024, 256, dtype=BF16),
)


def prepare(rank, own, items, accum, pair, sib):
    return pl.pallas_call(
        prepare_kernel,
        out_shape=USER_SHAPES + (struct(2, 256, EDGE),),
        in_specs=[SMEM] + [VMEM] * 5,
        out_specs=(VMEM,) * 6,
        scratch_shapes=[pltpu.VMEM((256, 1024), F32)],
        compiler_params=PARAMS,
        cost_estimate=cost(0),
        name="prepare",
    )(rank, own, items, accum, pair, sib)


def add_tile(rank, place, pieces, top, sums):
    for k, piece in zip((0, 2, 1, 3), pieces):
        start = pl.multiple_of(top + (rank ^ k) * QUARTER, QUARTER)
        sums[pl.ds(start, QUARTER), :] += piece[place].astype(F32)


def sum_kernel(stratum, rank, count, user, item, *rest):
    pieces, sums = rest[:4], rest[4]
    mine = rank[0]
    sums[...] = jnp.zeros_like(sums)
    for p in range(SLOTS):
        slot = stratum * SLOTS + p

        @pl.when(p < count[0, stratum])
        def _():
            target = sums.at[item[0, slot] ^ mine]
            add_tile(mine, p, pieces, user[0, slot] * EDGE, target)


def sum_tiles(stratum, scalars, pieces):
    return pl.pallas_call(
        functools.partial(sum_kernel, stratum),
        out_shape=struct(4, 1024, EDGE),
        in_specs=[SMEM] * 4 + [VMEM] * 4,
        out_specs=VMEM,
        compiler_params=PARAMS,
        cost_estimate=cost(30 if stratum == 0 else 0),
        name=f"sum_tiles{stratum}",
    )(*scalars[:4], *pieces)


def item_kernel(stratum, rank, counts, uh, ul, uth, utl, state, sums, *rest):
    *outs, errors = rest
    mine = rank[0]
    items = state[0]
    vh, vl = split(items)
    both = jnp.concatenate([vh, vl], axis=1)
    grad = jnp.zeros_like(items)
    for first in range(0, 1024, CHUNK):
        rows = slice(first, first + CHUNK)
        wide = dot(uth[rows, :], both)
        predicted = wide[:, :EDGE] + wide[:, EDGE:] + dot(utl[rows, :], vh)
        parts = []
        for k in range(CHUNK // EDGE):
            top = first + k * EDGE
            live = counts[stratum, top // EDGE * 4 + mine]
            parts.append(sums[0, top : top + EDGE, :] - live * predicted[k * EDGE : (k + 1) * EDGE])
        eh, el = split(jnp.concatenate(parts, axis=0))
        es = jnp.concatenate([eh, el], axis=1)
        errors[rows, :] = es
        wide = dot(uh[:, rows], es)
        grad += wide[:, :EDGE] + wide[:, EDGE:] + dot(ul[:, rows], eh)
    grad = grad - DECAY * items
    accum = state[1] + grad * grad
    items = items + LR_ITEM * grad / jnp.sqrt(accum)
    if stratum < STRATA - 1:
        outs[0][0] = items
        outs[0][1] = accum
    else:
        near, far, spot = outs
        spot[0] = items
        spot[1] = accum
        for j, rows in enumerate(group_rows(mine)):
            target = far if j % 2 else near
            for k in range(2):
                target[j // 2, k] = spot[k, rows, :]


def item_step(stratum, scalars, users, state, sums):
    if stratum < STRATA - 1:
        out = (struct(2, 256, EDGE),)
    else:
        out = (struct(2, 2, 64, EDGE), struct(2, 2, 64, EDGE), struct(2, 256, EDGE))
    return pl.pallas_call(
        functools.partial(item_kernel, stratum),
        out_shape=out + (struct(1024, 2 * EDGE, dtype=BF16),),
        in_specs=[SMEM] * 2 + [VMEM] * 6,
        out_specs=(VMEM,) * (len(out) + 1),
        compiler_params=PARAMS,
        cost_estimate=cost(12),
        name=f"item_step{stratum}",
    )(scalars[0], scalars[4], *users[1:], state, sums)


def user_kernel(stratum, rank, counts, uf, uth, utl, v, vp, vs, vd, errors, sums, *outs):
    mine = rank[0]
    last = stratum == STRATA - 1
    others = jnp.concatenate([vp[...], vs[...], vd[...]], axis=1)
    oh, ol = split(others)
    if last:
        rows = pl.ds(pl.multiple_of(mine * 64, 64), 64)
        kept = jnp.concatenate([x[rows, :] for x in (v, vp, vs, vd)], axis=1)
        kh, kl = split(kept)
    else:
        rows = slice(None)
        vh, vl = split(v[...])
        kh = jnp.concatenate([vh, oh], axis=1)
        kl = jnp.concatenate([vl, ol], axis=1)
    for first in range(0, 1024, CHUNK):
        span = slice(first, first + CHUNK)
        predicted = three(dot, (uth[span, :], utl[span, :]), (oh, ol))
        lines = []
        for k in range(CHUNK // EDGE):
            top = first + k * EDGE
            line = []
            for j, other in enumerate((2, 1, 3)):
                live = counts[stratum, top // EDGE * 4 + (mine ^ other)]
                part = predicted[k * EDGE : (k + 1) * EDGE, j * EDGE : (j + 1) * EDGE]
                line.append(sums[other, top : top + EDGE, :] - live * part)
            lines.append(jnp.concatenate(line, axis=1))
        eh, el = split(jnp.concatenate(lines, axis=0))
        eh = jnp.concatenate([errors[span, :EDGE], eh], axis=1)
        el = jnp.concatenate([errors[span, EDGE:], el], axis=1)
        grad = three(dot_nt, (kh, kl), (eh, el))
        old = uf[rows, span]
        new = old + LR_USER * (grad - DECAY * old)
        if last:
            outs[0][:, span] = new
        else:
            store_users(new, first, first + CHUNK, *outs)


def user_step(stratum, scalars, users, v, others, errors, sums):
    last = stratum == STRATA - 1
    return pl.pallas_call(
        functools.partial(user_kernel, stratum),
        out_shape=(struct(64, 1024),) if last else USER_SHAPES,
        in_specs=[SMEM] * 2 + [VMEM] * 9,
        out_specs=(VMEM,) * (1 if last else 5),
        compiler_params=PARAMS,
        cost_estimate=cost(0),
        name=f"user_step{stratum}",
    )(scalars[0], scalars[4], users[0], users[3], users[4], v, *others, errors, sums)


def place_kernel(rank, near, far, other, items, accum):
    mine = rank[0]
    for k, part in enumerate((near.at[0], other.at[0], far.at[0], other.at[1])):
        cols = pl.ds(pl.multiple_of((mine ^ k) * EDGE, EDGE), EDGE)
        items[:, cols] = part[0]
        accum[:, cols] = part[1]


def place_state(rank, near, far, other):
    return pl.pallas_call(
        place_kernel,
        out_shape=(struct(64, 512), struct(64, 512)),
        in_specs=[SMEM] + [VMEM] * 3,
        out_specs=(VMEM, VMEM),
        compiler_params=PARAMS,
        cost_estimate=cost(2),
        name="place_state",
    )(rank, near, far, other)


def exchange(x, by):
    return lax.ppermute(x, "rank", [(r, r ^ by) for r in range(4)])


def exchange_halves(x):
    return jnp.concatenate([exchange(x[:128], 1), exchange(x[128:], 1)])


def send_on(x, by):
    n = lax.axis_size("blk")
    return lax.ppermute(
        x,
        ("blk", "rank"),
        [(o * 4 + r, (o + 1) % n * 4 + (r ^ by)) for o in range(n) for r in range(4)],
    )


def body(
    ratings,
    send_list,
    plan,
    block_count,
    block_user,
    block_item,
    user_factors,
    item_factors,
    item_accum,
):
    rank = lax.axis_index("rank").astype(jnp.int32).reshape(1)
    quarter = (user_factors, item_factors, item_accum)
    offered, counts = offer(rank, block_count, block_user, block_item, *quarter)
    pair = exchange(offered, 2)
    scalars = (rank, block_count, block_user, block_item, counts)

    outgoing = gather_outgoing(rank, send_list, ratings)
    received = lax.all_to_all(outgoing, "blk", split_axis=0, concat_axis=0, tiled=True)

    tiles = list(order_received(plan, received))
    first = tiles[0]
    first_pair = exchange(first, 2)
    first_sib = exchange(first, 1)

    pair, tiles[2] = lax.optimization_barrier((pair, tiles[2]))
    sib = exchange(pack(rank, *quarter, pair), 1)
    *users, state = prepare(rank, *quarter, pair, sib)

    tiles[1], first_pair = lax.optimization_barrier((tiles[1], first_pair))
    next_pair = exchange(tiles[1], 2)
    sums = sum_tiles(0, scalars, (first, first_pair, first_sib, exchange(first_pair, 1)))
    for stratum in range(STRATA):
        last = stratum == STRATA - 1
        *out, errors = item_step(stratum, scalars, users, state, sums)
        v = state[0]
        vp = exchange(v, 2)
        if last:
            near = send_on(out[0], 0)
            far = send_on(out[1], 2)
            late, errors = lax.optimization_barrier((v, errors))
        else:
            state = send_on(out[0], 0)
            late, own, errors = lax.optimization_barrier((v, tiles[stratum + 1], errors))
            next_sib = exchange(own, 1)
            next_pair, errors = lax.optimization_barrier((next_pair, errors))
            next_diag = exchange(next_pair, 1)
        if last:
            late, vp, errors = lax.optimization_barrier((late, vp, errors))
            vs, vd = exchange_halves(late), exchange_halves(vp)
        else:
            vs = exchange(late, 1)
            vp, errors = lax.optimization_barrier((vp, errors))
            vd = exchange(vp, 1)
        if not last:
            after = (tiles[stratum + 1], next_pair, next_sib, next_diag)
            if stratum < 2:
                tiles[stratum + 2], vd = lax.optimization_barrier((tiles[stratum + 2], vd))
                next_pair = exchange(tiles[stratum + 2], 2)
            vs, vd, after, errors = lax.optimization_barrier((vs, vd, after, errors))
        else:
            vs, vd, errors = lax.optimization_barrier((vs, vd, errors))
        users = user_step(stratum, scalars, users, v, (vp, vs, vd), errors, sums)
        if not last:
            sums = sum_tiles(stratum + 1, scalars, after)
            state, users, sums = lax.optimization_barrier((state, users, sums))
    near, far, users_out = lax.optimization_barrier((near, far, users[0]))
    other = exchange(jnp.stack([near[1], far[1]]), 1)
    items_out, accum_out = place_state(rank, near, far, other)
    return users_out, items_out, accum_out


def solution(mesh):
    placed = (
        P("blk", None, None),
        P("blk", None),
        P("blk", None),
        P("blk", None),
        P("blk", None),
        P("blk", None),
        P("rank", "blk"),
        P("rank", "blk"),
        P("rank", "blk"),
    )
    return jax.shard_map(
        body,
        mesh=mesh,
        in_specs=placed,
        out_specs=(P("rank", "blk"), P("rank", "blk"), P("rank", "blk")),
        check_vma=False,
    )
```

```python
import functools

import jax
import jax.numpy as jnp
from jax import lax
from jax.experimental import pallas as pl
from jax.experimental.pallas import tpu as pltpu
from jax.sharding import PartitionSpec as P

LR_USER = 0.01
LR_ITEM = 0.05
DECAY = 0.05
F32 = jnp.float32
BF16 = jnp.bfloat16
EDGE = 128
SLOTS = 16
STRATA = 4
QUARTER = 32
CHUNK = 1024
VMEM = pl.BlockSpec(memory_space=pltpu.VMEM)
SMEM = pl.BlockSpec(memory_space=pltpu.SMEM)
HBM = pl.BlockSpec(memory_space=pltpu.HBM)
PARAMS = pltpu.CompilerParams(vmem_limit_bytes=16 * 2**20)


def cost(time):
    return pl.CostEstimate(flops=10**9 * time, bytes_accessed=3 * 10**6 * time, transcendentals=0)


def split(x):
    high = x.astype(BF16)
    return high, (x - high.astype(F32)).astype(BF16)


def dot(a, b):
    return jnp.dot(a, b, preferred_element_type=F32)


def dot_nt(a, b):
    return lax.dot_general(a, b, (((1,), (1,)), ((), ())), preferred_element_type=F32)


def three(product, a, b):
    return product(a[0], b[0]) + product(a[0], b[1]) + product(a[1], b[0])


def struct(*shape, dtype=F32):
    return jax.ShapeDtypeStruct(shape, dtype)


def gather_kernel(rank, routes, ratings, out, places, sems):
    fetch = pltpu.make_async_copy(routes, places, sems.at[0])
    fetch.start()
    fetch.wait()
    row = pl.multiple_of(rank[0] * QUARTER, QUARTER)
    for d in range(64):
        pltpu.make_async_copy(
            ratings.at[places[0, d], pl.ds(row, QUARTER), :], out.at[d], sems.at[1]
        ).start()
    pltpu.make_async_copy(out, out, sems.at[1]).wait()


def gather_outgoing(rank, routes, ratings):
    return pl.pallas_call(
        gather_kernel,
        out_shape=struct(64, QUARTER, EDGE, dtype=BF16),
        in_specs=[SMEM, HBM, HBM],
        out_specs=VMEM,
        scratch_shapes=[pltpu.SMEM((1, 64), jnp.int32), pltpu.SemaphoreType.DMA((2,))],
        compiler_params=pltpu.CompilerParams(vmem_limit_bytes=65 * 10**6),
        cost_estimate=cost(2),
        name="gather_outgoing",
    )(rank, routes, ratings)


def order_kernel(plan, received, *outs):
    for stratum, out in enumerate(outs):
        for p in range(SLOTS):
            out[p] = received[plan[0, stratum * SLOTS + p]]


def order_received(plan, received):
    return pl.pallas_call(
        order_kernel,
        out_shape=(struct(SLOTS, QUARTER, EDGE, dtype=BF16),) * STRATA,
        in_specs=[SMEM, VMEM],
        out_specs=(VMEM,) * STRATA,
        compiler_params=PARAMS,
        cost_estimate=cost(4),
        name="order_received",
    )(plan, received)


def block_of(ref, block):
    return ref[:, pl.ds(pl.multiple_of(block * EDGE, EDGE), EDGE)]


def store_users(uf, first, last, uf_ref, uh, ul, uth, utl):
    cols = slice(first, last)
    high, low = split(uf)
    uf_ref[:, cols] = uf
    uh[:, cols] = high
    ul[:, cols] = low
    turned = uf.T
    high, low = split(turned)
    uth[cols, :] = high
    utl[cols, :] = low


def block_held(stratum, rank):
    return rank ^ (2 if stratum % 2 else 0)


def group_rows(rank):
    return [pl.ds(pl.multiple_of((rank ^ k) * 64, 64), 64) for k in (0, 2, 1, 3)]


def offer_kernel(rank, count, user, item, users, items, accum, out, counts):
    for s in range(STRATA):
        for k in range(32):
            counts[s, k] = 0.0
        for p in range(SLOTS):
            slot = s * SLOTS + p
            where = user[0, slot] * 4 + item[0, slot]
            counts[s, where] += jnp.where(p < count[0, s], 1.0, 0.0)
    out[:, :1024] = users[...]
    for k, source in enumerate((items, accum)):
        for j in range(2):
            start = 1024 + (2 * k + j) * EDGE
            out[:, start : start + EDGE] = block_of(source, rank[0] ^ 2 ^ j)


def offer(rank, count, user, item, users, items, accum):
    return pl.pallas_call(
        offer_kernel,
        out_shape=(struct(64, 1536), struct(STRATA, 32)),
        in_specs=[SMEM] * 4 + [VMEM] * 3,
        out_specs=(VMEM, SMEM),
        compiler_params=PARAMS,
        cost_estimate=cost(2),
        name="offer",
    )(rank, count, user, item, users, items, accum)


def pack_kernel(rank, users, items, accum, pair, out):
    sibling = rank[0] ^ 1
    out[0, :, :1024] = users[...]
    out[1, :, :1024] = pair[:, :1024]
    for k, source in enumerate((items, accum)):
        cols = slice(1024 + k * EDGE, 1024 + (k + 1) * EDGE)
        out[0, :, cols] = block_of(source, sibling)
        start = 1024 + (2 * k + 1) * EDGE
        out[1, :, cols] = pair[:, start : start + EDGE]


def pack(rank, users, items, accum, pair):
    return pl.pallas_call(
        pack_kernel,
        out_shape=struct(2, 64, 1280),
        in_specs=[SMEM] + [VMEM] * 4,
        out_specs=VMEM,
        compiler_params=PARAMS,
        cost_estimate=cost(0),
        name="pack",
    )(rank, users, items, accum, pair)


def prepare_kernel(
    rank, own, items, accum, pair, sib, uf, uh, ul, uth, utl, state, users
):
    mine = rank[0]
    places = group_rows(mine)
    parts = (own, pair.at[:, :1024], sib.at[0, :, :1024], sib.at[1, :, :1024])
    for place, part in zip(places, parts):
        users[place, :] = part[...]
    for first in range(0, 1024, CHUNK):
        last = first + CHUNK
        store_users(users[:, first:last], first, last, uf, uh, ul, uth, utl)
    for k, own_part in enumerate((items, accum)):
        state[k, places[0], :] = block_of(own_part, mine)
        start = 1024 + 2 * k * EDGE
        state[k, places[1], :] = pair[:, start : start + EDGE]
        for j in range(2):
            start = 1024 + EDGE * k
            state[k, places[2 + j], :] = sib[j, :, start : start + EDGE]


USER_SHAPES = (
    struct(256, 1024),
    struct(256, 1024, dtype=BF16),
    struct(256, 1024, dtype=BF16),
    struct(1024, 256, dtype=BF16),
    struct(1024, 256, dtype=BF16),
)


def prepare(rank, own, items, accum, pair, sib):
    return pl.pallas_call(
        prepare_kernel,
        out_shape=USER_SHAPES + (struct(2, 256, EDGE),),
        in_specs=[SMEM] + [VMEM] * 5,
        out_specs=(VMEM,) * 6,
        scratch_shapes=[pltpu.VMEM((256, 1024), F32)],
        compiler_params=PARAMS,
        cost_estimate=cost(0),
        name="prepare",
    )(rank, own, items, accum, pair, sib)


def add_tile(rank, place, pieces, top, sums):
    for k, piece in zip((0, 2, 1, 3), pieces):
        start = pl.multiple_of(top + (rank ^ k) * QUARTER, QUARTER)
        sums[pl.ds(start, QUARTER), :] += piece[place].astype(F32)


def sum_kernel(stratum, rank, count, user, item, *rest):
    pieces, sums = rest[:4], rest[4]
    mine = rank[0]
    sums[...] = jnp.zeros_like(sums)
    for p in range(SLOTS):
        slot = stratum * SLOTS + p

        @pl.when(p < count[0, stratum])
        def _():
            target = sums.at[item[0, slot] ^ block_held(stratum, mine)]
            add_tile(mine, p, pieces, user[0, slot] * EDGE, target)


def sum_tiles(stratum, scalars, pieces):
    return pl.pallas_call(
        functools.partial(sum_kernel, stratum),
        out_shape=struct(4, 1024, EDGE),
        in_specs=[SMEM] * 4 + [VMEM] * 4,
        out_specs=VMEM,
        compiler_params=PARAMS,
        cost_estimate=cost(30 if stratum == 0 else 0),
        name=f"sum_tiles{stratum}",
    )(*scalars[:4], *pieces)


def item_kernel(stratum, rank, counts, uh, ul, uth, utl, state, sums, *rest):
    *outs, errors = rest
    mine = rank[0]
    items = state[0]
    vh, vl = split(items)
    both = jnp.concatenate([vh, vl], axis=1)
    grad = jnp.zeros_like(items)
    for first in range(0, 1024, CHUNK):
        rows = slice(first, first + CHUNK)
        wide = dot(uth[rows, :], both)
        predicted = wide[:, :EDGE] + wide[:, EDGE:] + dot(utl[rows, :], vh)
        parts = []
        for k in range(CHUNK // EDGE):
            top = first + k * EDGE
            live = counts[stratum, top // EDGE * 4 + block_held(stratum, mine)]
            parts.append(sums[0, top : top + EDGE, :] - live * predicted[k * EDGE : (k + 1) * EDGE])
        eh, el = split(jnp.concatenate(parts, axis=0))
        es = jnp.concatenate([eh, el], axis=1)
        errors[rows, :] = es
        wide = dot(uh[:, rows], es)
        grad += wide[:, :EDGE] + wide[:, EDGE:] + dot(ul[:, rows], eh)
    grad = grad - DECAY * items
    accum = state[1] + grad * grad
    items = items + LR_ITEM * grad / jnp.sqrt(accum)
    if stratum < STRATA - 1:
        outs[0][0] = items
        outs[0][1] = accum
    else:
        near, far, spot = outs
        spot[0] = items
        spot[1] = accum
        for j, rows in enumerate(group_rows(mine)):
            target = far if j % 2 else near
            for k in range(2):
                target[j // 2, k] = spot[k, rows, :]


def item_step(stratum, scalars, users, state, sums):
    if stratum < STRATA - 1:
        out = (struct(2, 256, EDGE),)
    else:
        out = (struct(2, 2, 64, EDGE), struct(2, 2, 64, EDGE), struct(2, 256, EDGE))
    return pl.pallas_call(
        functools.partial(item_kernel, stratum),
        out_shape=out + (struct(1024, 2 * EDGE, dtype=BF16),),
        in_specs=[SMEM] * 2 + [VMEM] * 6,
        out_specs=(VMEM,) * (len(out) + 1),
        compiler_params=PARAMS,
        cost_estimate=cost(12),
        name=f"item_step{stratum}",
    )(scalars[0], scalars[4], *users[1:], state, sums)


def user_kernel(stratum, rank, counts, uf, uth, utl, v, vp, vs, vd, errors, sums, *outs):
    mine = rank[0]
    last = stratum == STRATA - 1
    others = jnp.concatenate([vp[...], vs[...], vd[...]], axis=1)
    oh, ol = split(others)
    if last:
        rows = pl.ds(pl.multiple_of(mine * 64, 64), 64)
        kept = jnp.concatenate([x[rows, :] for x in (v, vp, vs, vd)], axis=1)
        kh, kl = split(kept)
    else:
        rows = slice(None)
        vh, vl = split(v[...])
        kh = jnp.concatenate([vh, oh], axis=1)
        kl = jnp.concatenate([vl, ol], axis=1)
    for first in range(0, 1024, CHUNK):
        span = slice(first, first + CHUNK)
        predicted = three(dot, (uth[span, :], utl[span, :]), (oh, ol))
        lines = []
        for k in range(CHUNK // EDGE):
            top = first + k * EDGE
            line = []
            for j, other in enumerate((2, 1, 3)):
                live = counts[stratum, top // EDGE * 4 + (block_held(stratum, mine) ^ other)]
                part = predicted[k * EDGE : (k + 1) * EDGE, j * EDGE : (j + 1) * EDGE]
                line.append(sums[other, top : top + EDGE, :] - live * part)
            lines.append(jnp.concatenate(line, axis=1))
        eh, el = split(jnp.concatenate(lines, axis=0))
        eh = jnp.concatenate([errors[span, :EDGE], eh], axis=1)
        el = jnp.concatenate([errors[span, EDGE:], el], axis=1)
        grad = three(dot_nt, (kh, kl), (eh, el))
        old = uf[rows, span]
        new = old + LR_USER * (grad - DECAY * old)
        if last:
            outs[0][:, span] = new
        else:
            store_users(new, first, first + CHUNK, *outs)


def user_step(stratum, scalars, users, v, others, errors, sums):
    last = stratum == STRATA - 1
    return pl.pallas_call(
        functools.partial(user_kernel, stratum),
        out_shape=(struct(64, 1024),) if last else USER_SHAPES,
        in_specs=[SMEM] * 2 + [VMEM] * 9,
        out_specs=(VMEM,) * (1 if last else 5),
        compiler_params=PARAMS,
        cost_estimate=cost(0),
        name=f"user_step{stratum}",
    )(scalars[0], scalars[4], users[0], users[3], users[4], v, *others, errors, sums)


def place_kernel(rank, near, far, other, items, accum):
    mine = rank[0]
    for k, part in enumerate((near.at[0], other.at[0], far.at[0], other.at[1])):
        cols = pl.ds(pl.multiple_of((mine ^ k ^ 2) * EDGE, EDGE), EDGE)
        items[:, cols] = part[0]
        accum[:, cols] = part[1]


def place_state(rank, near, far, other):
    return pl.pallas_call(
        place_kernel,
        out_shape=(struct(64, 512), struct(64, 512)),
        in_specs=[SMEM] + [VMEM] * 3,
        out_specs=(VMEM, VMEM),
        compiler_params=PARAMS,
        cost_estimate=cost(2),
        name="place_state",
    )(rank, near, far, other)


def exchange(x, by):
    return lax.ppermute(x, "rank", [(r, r ^ by) for r in range(4)])


def exchange_halves(x):
    return jnp.concatenate([exchange(x[:128], 1), exchange(x[128:], 1)])


def send_on(x, by):
    n = lax.axis_size("blk")
    return lax.ppermute(
        x,
        ("blk", "rank"),
        [(o * 4 + r, (o + 1) % n * 4 + (r ^ by)) for o in range(n) for r in range(4)],
    )


def body(
    ratings,
    send_list,
    plan,
    block_count,
    block_user,
    block_item,
    user_factors,
    item_factors,
    item_accum,
):
    rank = lax.axis_index("rank").astype(jnp.int32).reshape(1)
    quarter = (user_factors, item_factors, item_accum)
    offered, counts = offer(rank, block_count, block_user, block_item, *quarter)
    pair = exchange(offered, 2)
    scalars = (rank, block_count, block_user, block_item, counts)

    outgoing = gather_outgoing(rank, send_list, ratings)
    received = lax.all_to_all(outgoing, "blk", split_axis=0, concat_axis=0, tiled=True)

    tiles = list(order_received(plan, received))
    first = tiles[0]
    first_pair = exchange(first, 2)
    first_sib = exchange(first, 1)

    pair, tiles[2] = lax.optimization_barrier((pair, tiles[2]))
    sib = exchange(pack(rank, *quarter, pair), 1)
    *users, state = prepare(rank, *quarter, pair, sib)

    tiles[1], first_pair = lax.optimization_barrier((tiles[1], first_pair))
    next_pair = exchange(tiles[1], 2)
    sums = sum_tiles(0, scalars, (first, first_pair, first_sib, exchange(first_pair, 1)))
    for stratum in range(STRATA):
        last = stratum == STRATA - 1
        *out, errors = item_step(stratum, scalars, users, state, sums)
        v = state[0]
        vp = exchange(v, 2)
        if last:
            near = send_on(out[0], 0)
            far = send_on(out[1], 2)
            late, errors = lax.optimization_barrier((v, errors))
        else:
            state = send_on(out[0], 2)
            late, own, errors = lax.optimization_barrier((v, tiles[stratum + 1], errors))
            next_sib = exchange(own, 1)
            next_pair, errors = lax.optimization_barrier((next_pair, errors))
            next_diag = exchange(next_pair, 1)
        if last:
            late, vp, errors = lax.optimization_barrier((late, vp, errors))
            vs, vd = exchange_halves(late), exchange_halves(vp)
        else:
            vs = exchange(late, 1)
            vp, errors = lax.optimization_barrier((vp, errors))
            vd = exchange(vp, 1)
        if not last:
            after = (tiles[stratum + 1], next_pair, next_sib, next_diag)
            if stratum < 2:
                tiles[stratum + 2], vd = lax.optimization_barrier((tiles[stratum + 2], vd))
                next_pair = exchange(tiles[stratum + 2], 2)
            vs, vd, after, errors = lax.optimization_barrier((vs, vd, after, errors))
        else:
            vs, vd, errors = lax.optimization_barrier((vs, vd, errors))
        users = user_step(stratum, scalars, users, v, (vp, vs, vd), errors, sums)
        if not last:
            sums = sum_tiles(stratum + 1, scalars, after)
            state, users, sums = lax.optimization_barrier((state, users, sums))
    near, far, users_out = lax.optimization_barrier((near, far, users[0]))
    other = exchange(jnp.stack([near[1], far[1]]), 1)
    items_out, accum_out = place_state(rank, near, far, other)
    return users_out, items_out, accum_out


def solution(mesh):
    placed = (
        P("blk", None, None),
        P("blk", None),
        P("blk", None),
        P("blk", None),
        P("blk", None),
        P("blk", None),
        P("rank", "blk"),
        P("rank", "blk"),
        P("rank", "blk"),
    )
    return jax.shard_map(
        body,
        mesh=mesh,
        in_specs=placed,
        out_specs=(P("rank", "blk"), P("rank", "blk"), P("rank", "blk")),
        check_vma=False,
    )
```

```python
import functools

import jax
import jax.numpy as jnp
from jax import lax
from jax.experimental import pallas as pl
from jax.experimental.pallas import tpu as pltpu
from jax.sharding import PartitionSpec as P

LR_USER = 0.01
LR_ITEM = 0.05
DECAY = 0.05
F32 = jnp.float32
BF16 = jnp.bfloat16
EDGE = 128
SLOTS = 16
STRATA = 4
QUARTER = 32
CHUNK = 1024
VMEM = pl.BlockSpec(memory_space=pltpu.VMEM)
SMEM = pl.BlockSpec(memory_space=pltpu.SMEM)
HBM = pl.BlockSpec(memory_space=pltpu.HBM)
PARAMS = pltpu.CompilerParams(vmem_limit_bytes=16 * 2**20)


def cost(time):
    return pl.CostEstimate(flops=10**9 * time, bytes_accessed=3 * 10**6 * time, transcendentals=0)


def split(x):
    high = x.astype(BF16)
    return high, (x - high.astype(F32)).astype(BF16)


def dot(a, b):
    return jnp.dot(a, b, preferred_element_type=F32)


def dot_nt(a, b):
    return lax.dot_general(a, b, (((1,), (1,)), ((), ())), preferred_element_type=F32)


def three(product, a, b):
    return product(a[0], b[0]) + product(a[0], b[1]) + product(a[1], b[0])


def struct(*shape, dtype=F32):
    return jax.ShapeDtypeStruct(shape, dtype)


def gather_kernel(rank, routes, ratings, out, places, sems):
    fetch = pltpu.make_async_copy(routes, places, sems.at[0])
    fetch.start()
    fetch.wait()
    row = pl.multiple_of(rank[0] * QUARTER, QUARTER)
    for d in range(64):
        pltpu.make_async_copy(
            ratings.at[places[0, d], pl.ds(row, QUARTER), :], out.at[d], sems.at[1]
        ).start()
    pltpu.make_async_copy(out, out, sems.at[1]).wait()


def gather_outgoing(rank, routes, ratings):
    return pl.pallas_call(
        gather_kernel,
        out_shape=struct(64, QUARTER, EDGE, dtype=BF16),
        in_specs=[SMEM, HBM, HBM],
        out_specs=VMEM,
        scratch_shapes=[pltpu.SMEM((1, 64), jnp.int32), pltpu.SemaphoreType.DMA((2,))],
        compiler_params=pltpu.CompilerParams(vmem_limit_bytes=65 * 10**6),
        cost_estimate=cost(2),
        name="gather_outgoing",
    )(rank, routes, ratings)


def order_kernel(plan, received, *outs):
    for stratum, out in enumerate(outs):
        for p in range(SLOTS):
            out[p] = received[plan[0, stratum * SLOTS + p]]


def order_received(plan, received):
    return pl.pallas_call(
        order_kernel,
        out_shape=(struct(SLOTS, QUARTER, EDGE, dtype=BF16),) * STRATA,
        in_specs=[SMEM, VMEM],
        out_specs=(VMEM,) * STRATA,
        compiler_params=PARAMS,
        cost_estimate=cost(4),
        name="order_received",
    )(plan, received)


def block_of(ref, block):
    return ref[:, pl.ds(pl.multiple_of(block * EDGE, EDGE), EDGE)]


def store_users(uf, first, last, uf_ref, uh, ul, uth, utl):
    cols = slice(first, last)
    high, low = split(uf)
    uf_ref[:, cols] = uf
    uh[:, cols] = high
    ul[:, cols] = low
    turned = uf.T
    high, low = split(turned)
    uth[cols, :] = high
    utl[cols, :] = low


def block_held(stratum, rank):
    return rank ^ (2 if stratum % 2 else 0)


def group_rows(rank):
    return [pl.ds(pl.multiple_of((rank ^ k) * 64, 64), 64) for k in (0, 2, 1, 3)]


def offer_kernel(rank, count, user, item, users, items, accum, out, counts):
    for s in range(STRATA):
        for k in range(32):
            counts[s, k] = 0.0
        for p in range(SLOTS):
            slot = s * SLOTS + p
            where = user[0, slot] * 4 + item[0, slot]
            counts[s, where] += jnp.where(p < count[0, s], 1.0, 0.0)
    out[:, :1024] = users[...]
    for k, source in enumerate((items, accum)):
        for j in range(2):
            start = 1024 + (2 * k + j) * EDGE
            out[:, start : start + EDGE] = block_of(source, rank[0] ^ 2 ^ j)


def offer(rank, count, user, item, users, items, accum):
    return pl.pallas_call(
        offer_kernel,
        out_shape=(struct(64, 1536), struct(STRATA, 32)),
        in_specs=[SMEM] * 4 + [VMEM] * 3,
        out_specs=(VMEM, SMEM),
        compiler_params=PARAMS,
        cost_estimate=cost(2),
        name="offer",
    )(rank, count, user, item, users, items, accum)


def pack_kernel(rank, users, items, accum, pair, out):
    sibling = rank[0] ^ 1
    out[0, :, :1024] = users[...]
    out[1, :, :1024] = pair[:, :1024]
    for k, source in enumerate((items, accum)):
        cols = slice(1024 + k * EDGE, 1024 + (k + 1) * EDGE)
        out[0, :, cols] = block_of(source, sibling)
        start = 1024 + (2 * k + 1) * EDGE
        out[1, :, cols] = pair[:, start : start + EDGE]


def pack(rank, users, items, accum, pair):
    return pl.pallas_call(
        pack_kernel,
        out_shape=struct(2, 64, 1280),
        in_specs=[SMEM] + [VMEM] * 4,
        out_specs=VMEM,
        compiler_params=PARAMS,
        cost_estimate=cost(0),
        name="pack",
    )(rank, users, items, accum, pair)


def prepare_kernel(
    rank, own, items, accum, pair, sib, uf, uh, ul, uth, utl, state, users
):
    mine = rank[0]
    places = group_rows(mine)
    parts = (own, pair.at[:, :1024], sib.at[0, :, :1024], sib.at[1, :, :1024])
    for place, part in zip(places, parts):
        users[place, :] = part[...]
    for first in range(0, 1024, CHUNK):
        last = first + CHUNK
        store_users(users[:, first:last], first, last, uf, uh, ul, uth, utl)
    for k, own_part in enumerate((items, accum)):
        state[k, places[0], :] = block_of(own_part, mine)
        start = 1024 + 2 * k * EDGE
        state[k, places[1], :] = pair[:, start : start + EDGE]
        for j in range(2):
            start = 1024 + EDGE * k
            state[k, places[2 + j], :] = sib[j, :, start : start + EDGE]


USER_SHAPES = (
    struct(256, 1024),
    struct(256, 1024, dtype=BF16),
    struct(256, 1024, dtype=BF16),
    struct(1024, 256, dtype=BF16),
    struct(1024, 256, dtype=BF16),
)


def prepare(rank, own, items, accum, pair, sib):
    return pl.pallas_call(
        prepare_kernel,
        out_shape=USER_SHAPES + (struct(2, 256, EDGE),),
        in_specs=[SMEM] + [VMEM] * 5,
        out_specs=(VMEM,) * 6,
        scratch_shapes=[pltpu.VMEM((256, 1024), F32)],
        compiler_params=PARAMS,
        cost_estimate=cost(0),
        name="prepare",
    )(rank, own, items, accum, pair, sib)


def add_tile(rank, place, pieces, top, sums):
    for k, piece in zip((0, 2, 1, 3), pieces):
        start = pl.multiple_of(top + (rank ^ k) * QUARTER, QUARTER)
        sums[pl.ds(start, QUARTER), :] += piece[place].astype(F32)


def sum_kernel(stratum, rank, count, user, item, *rest):
    pieces, sums = rest[:4], rest[4]
    mine = rank[0]
    sums[...] = jnp.zeros_like(sums)
    for p in range(SLOTS):
        slot = stratum * SLOTS + p

        @pl.when(p < count[0, stratum])
        def _():
            target = sums.at[item[0, slot] ^ block_held(stratum, mine)]
            add_tile(mine, p, pieces, user[0, slot] * EDGE, target)


def sum_tiles(stratum, scalars, pieces):
    return pl.pallas_call(
        functools.partial(sum_kernel, stratum),
        out_shape=struct(4, 1024, EDGE),
        in_specs=[SMEM] * 4 + [VMEM] * 4,
        out_specs=VMEM,
        compiler_params=PARAMS,
        cost_estimate=cost(30 if stratum == 0 else 0),
        name=f"sum_tiles{stratum}",
    )(*scalars[:4], *pieces)


def item_kernel(stratum, rank, counts, uh, ul, uth, utl, state, sums, *rest):
    *outs, errors = rest
    mine = rank[0]
    items = state[0]
    vh, vl = split(items)
    both = jnp.concatenate([vh, vl], axis=1)
    grad = jnp.zeros_like(items)
    for first in range(0, 1024, CHUNK):
        rows = slice(first, first + CHUNK)
        wide = dot(uth[rows, :], both)
        predicted = wide[:, :EDGE] + wide[:, EDGE:] + dot(utl[rows, :], vh)
        parts = []
        for k in range(CHUNK // EDGE):
            top = first + k * EDGE
            live = counts[stratum, top // EDGE * 4 + block_held(stratum, mine)]
            parts.append(sums[0, top : top + EDGE, :] - live * predicted[k * EDGE : (k + 1) * EDGE])
        eh, el = split(jnp.concatenate(parts, axis=0))
        es = jnp.concatenate([eh, el], axis=1)
        errors[rows, :] = es
        wide = dot(uh[:, rows], es)
        grad += wide[:, :EDGE] + wide[:, EDGE:] + dot(ul[:, rows], eh)
    grad = grad - DECAY * items
    accum = state[1] + grad * grad
    items = items + LR_ITEM * grad / jnp.sqrt(accum)
    if stratum < STRATA - 1:
        outs[0][0] = items
        outs[0][1] = accum
    else:
        near, far, spot = outs
        spot[0] = items
        spot[1] = accum
        for j, rows in enumerate(group_rows(mine)):
            target = far if j % 2 else near
            for k in range(2):
                target[j // 2, k] = spot[k, rows, :]


def item_step(stratum, scalars, users, state, sums):
    if stratum < STRATA - 1:
        out = (struct(2, 256, EDGE),)
    else:
        out = (struct(2, 2, 64, EDGE), struct(2, 2, 64, EDGE), struct(2, 256, EDGE))
    return pl.pallas_call(
        functools.partial(item_kernel, stratum),
        out_shape=out + (struct(1024, 2 * EDGE, dtype=BF16),),
        in_specs=[SMEM] * 2 + [VMEM] * 6,
        out_specs=(VMEM,) * (len(out) + 1),
        compiler_params=PARAMS,
        cost_estimate=cost(12),
        name=f"item_step{stratum}",
    )(scalars[0], scalars[4], *users[1:], state, sums)


def user_kernel(stratum, rank, counts, uf, uth, utl, v, vp, vs, vd, errors, sums, *outs):
    mine = rank[0]
    last = stratum == STRATA - 1
    others = jnp.concatenate([vp[...], vs[...], vd[...]], axis=1)
    oh, ol = split(others)
    if last:
        rows = pl.ds(pl.multiple_of(mine * 64, 64), 64)
        kept = jnp.concatenate([x[rows, :] for x in (v, vp, vs, vd)], axis=1)
        kh, kl = split(kept)
    else:
        rows = slice(None)
        vh, vl = split(v[...])
        kh = jnp.concatenate([vh, oh], axis=1)
        kl = jnp.concatenate([vl, ol], axis=1)
    for first in range(0, 1024, CHUNK):
        span = slice(first, first + CHUNK)
        predicted = three(dot, (uth[span, :], utl[span, :]), (oh, ol))
        lines = []
        for k in range(CHUNK // EDGE):
            top = first + k * EDGE
            line = []
            for j, other in enumerate((2, 1, 3)):
                live = counts[stratum, top // EDGE * 4 + (block_held(stratum, mine) ^ other)]
                part = predicted[k * EDGE : (k + 1) * EDGE, j * EDGE : (j + 1) * EDGE]
                line.append(sums[other, top : top + EDGE, :] - live * part)
            lines.append(jnp.concatenate(line, axis=1))
        eh, el = split(jnp.concatenate(lines, axis=0))
        eh = jnp.concatenate([errors[span, :EDGE], eh], axis=1)
        el = jnp.concatenate([errors[span, EDGE:], el], axis=1)
        grad = three(dot_nt, (kh, kl), (eh, el))
        old = uf[rows, span]
        new = old + LR_USER * (grad - DECAY * old)
        if last:
            outs[0][:, span] = new
        else:
            store_users(new, first, first + CHUNK, *outs)


def user_step(stratum, scalars, users, v, others, errors, sums):
    last = stratum == STRATA - 1
    return pl.pallas_call(
        functools.partial(user_kernel, stratum),
        out_shape=(struct(64, 1024),) if last else USER_SHAPES,
        in_specs=[SMEM] * 2 + [VMEM] * 9,
        out_specs=(VMEM,) * (1 if last else 5),
        compiler_params=PARAMS,
        cost_estimate=cost(0),
        name=f"user_step{stratum}",
    )(scalars[0], scalars[4], users[0], users[3], users[4], v, *others, errors, sums)


def place_kernel(rank, near, far, other, items, accum):
    mine = rank[0]
    for k, part in enumerate((near.at[0], other.at[0], far.at[0], other.at[1])):
        cols = pl.ds(pl.multiple_of((mine ^ k ^ 2) * EDGE, EDGE), EDGE)
        items[:, cols] = part[0]
        accum[:, cols] = part[1]


def place_state(rank, near, far, other):
    return pl.pallas_call(
        place_kernel,
        out_shape=(struct(64, 512), struct(64, 512)),
        in_specs=[SMEM] + [VMEM] * 3,
        out_specs=(VMEM, VMEM),
        compiler_params=PARAMS,
        cost_estimate=cost(2),
        name="place_state",
    )(rank, near, far, other)


def exchange(x, by):
    return lax.ppermute(x, "rank", [(r, r ^ by) for r in range(4)])


def exchange_halves(x):
    return jnp.concatenate([exchange(x[:128], 1), exchange(x[128:], 1)])


def send_on(x, by):
    n = lax.axis_size("blk")
    return lax.ppermute(
        x,
        ("blk", "rank"),
        [(o * 4 + r, (o + 1) % n * 4 + (r ^ by)) for o in range(n) for r in range(4)],
    )


def body(
    ratings,
    send_list,
    plan,
    block_count,
    block_user,
    block_item,
    user_factors,
    item_factors,
    item_accum,
):
    rank = lax.axis_index("rank").astype(jnp.int32).reshape(1)
    quarter = (user_factors, item_factors, item_accum)
    offered, counts = offer(rank, block_count, block_user, block_item, *quarter)
    pair = exchange(offered, 2)
    scalars = (rank, block_count, block_user, block_item, counts)

    outgoing = gather_outgoing(rank, send_list, ratings)
    received = lax.all_to_all(outgoing, "blk", split_axis=0, concat_axis=0, tiled=True)

    tiles = list(order_received(plan, received))
    first = tiles[0]
    first_pair = exchange(first, 2)
    first_sib = exchange(first, 1)

    pair, tiles[2] = lax.optimization_barrier((pair, tiles[2]))
    sib = exchange(pack(rank, *quarter, pair), 1)
    *users, state = prepare(rank, *quarter, pair, sib)

    tiles[1], first_pair, state = lax.optimization_barrier((tiles[1], first_pair, state))
    next_pair = exchange(tiles[1], 2)
    sums = sum_tiles(0, scalars, (first, first_pair, first_sib, exchange(first_pair, 1)))
    for stratum in range(STRATA):
        last = stratum == STRATA - 1
        *out, errors = item_step(stratum, scalars, users, state, sums)
        v = state[0]
        vp = exchange(v, 2)
        if last:
            near = send_on(out[0], 0)
            far = send_on(out[1], 2)
            late, errors = lax.optimization_barrier((v, errors))
        else:
            state = send_on(out[0], 2)
            late, own, errors = lax.optimization_barrier((v, tiles[stratum + 1], errors))
            next_sib = exchange(own, 1)
            next_pair, errors = lax.optimization_barrier((next_pair, errors))
            next_diag = exchange(next_pair, 1)
        if last:
            late, vp, errors = lax.optimization_barrier((late, vp, errors))
            vs, vd = exchange_halves(late), exchange_halves(vp)
        else:
            vs = exchange(late, 1)
            vp, errors = lax.optimization_barrier((vp, errors))
            vd = exchange(vp, 1)
        if not last:
            after = (tiles[stratum + 1], next_pair, next_sib, next_diag)
            if stratum < 2:
                tiles[stratum + 2], vd = lax.optimization_barrier((tiles[stratum + 2], vd))
                next_pair = exchange(tiles[stratum + 2], 2)
            vs, vd, after, errors = lax.optimization_barrier((vs, vd, after, errors))
        else:
            vs, vd, errors = lax.optimization_barrier((vs, vd, errors))
        users = user_step(stratum, scalars, users, v, (vp, vs, vd), errors, sums)
        if not last:
            sums = sum_tiles(stratum + 1, scalars, after)
            state, users, sums = lax.optimization_barrier((state, users, sums))
    near, far, users_out = lax.optimization_barrier((near, far, users[0]))
    other = exchange(jnp.stack([near[1], far[1]]), 1)
    items_out, accum_out = place_state(rank, near, far, other)
    return users_out, items_out, accum_out


def solution(mesh):
    placed = (
        P("blk", None, None),
        P("blk", None),
        P("blk", None),
        P("blk", None),
        P("blk", None),
        P("blk", None),
        P("rank", "blk"),
        P("rank", "blk"),
        P("rank", "blk"),
    )
    return jax.shard_map(
        body,
        mesh=mesh,
        in_specs=placed,
        out_specs=(P("rank", "blk"), P("rank", "blk"), P("rank", "blk")),
        check_vma=False,
    )
```

```python
import functools

import jax
import jax.numpy as jnp
from jax import lax
from jax.experimental import pallas as pl
from jax.experimental.pallas import tpu as pltpu
from jax.sharding import PartitionSpec as P

LR_USER = 0.01
LR_ITEM = 0.05
DECAY = 0.05
F32 = jnp.float32
BF16 = jnp.bfloat16
EDGE = 128
SLOTS = 16
STRATA = 4
QUARTER = 32
CHUNK = 1024
VMEM = pl.BlockSpec(memory_space=pltpu.VMEM)
SMEM = pl.BlockSpec(memory_space=pltpu.SMEM)
HBM = pl.BlockSpec(memory_space=pltpu.HBM)
PARAMS = pltpu.CompilerParams(vmem_limit_bytes=16 * 2**20)


def cost(time):
    return pl.CostEstimate(flops=10**9 * time, bytes_accessed=3 * 10**6 * time, transcendentals=0)


def split(x):
    high = x.astype(BF16)
    return high, (x - high.astype(F32)).astype(BF16)


def dot(a, b):
    return jnp.dot(a, b, preferred_element_type=F32)


def dot_nt(a, b):
    return lax.dot_general(a, b, (((1,), (1,)), ((), ())), preferred_element_type=F32)


def three(product, a, b):
    return product(a[0], b[0]) + product(a[0], b[1]) + product(a[1], b[0])


def struct(*shape, dtype=F32):
    return jax.ShapeDtypeStruct(shape, dtype)


def gather_kernel(rank, routes, ratings, out, places, sems):
    fetch = pltpu.make_async_copy(routes, places, sems.at[0])
    fetch.start()
    fetch.wait()
    row = pl.multiple_of(rank[0] * QUARTER, QUARTER)
    for d in range(64):
        pltpu.make_async_copy(
            ratings.at[places[0, d], pl.ds(row, QUARTER), :], out.at[d], sems.at[1]
        ).start()
    pltpu.make_async_copy(out, out, sems.at[1]).wait()


def gather_outgoing(rank, routes, ratings):
    return pl.pallas_call(
        gather_kernel,
        out_shape=struct(64, QUARTER, EDGE, dtype=BF16),
        in_specs=[SMEM, HBM, HBM],
        out_specs=VMEM,
        scratch_shapes=[pltpu.SMEM((1, 64), jnp.int32), pltpu.SemaphoreType.DMA((2,))],
        compiler_params=pltpu.CompilerParams(vmem_limit_bytes=65 * 10**6),
        cost_estimate=cost(2),
        name="gather_outgoing",
    )(rank, routes, ratings)


def order_kernel(plan, received, *outs):
    for stratum, out in enumerate(outs):
        for p in range(SLOTS):
            out[p] = received[plan[0, stratum * SLOTS + p]]


def order_received(plan, received):
    return pl.pallas_call(
        order_kernel,
        out_shape=(struct(SLOTS, QUARTER, EDGE, dtype=BF16),) * STRATA,
        in_specs=[SMEM, VMEM],
        out_specs=(VMEM,) * STRATA,
        compiler_params=PARAMS,
        cost_estimate=cost(4),
        name="order_received",
    )(plan, received)


def block_of(ref, block):
    return ref[:, pl.ds(pl.multiple_of(block * EDGE, EDGE), EDGE)]


def store_users(uf, first, last, uf_ref, uh, ul, uth, utl):
    cols = slice(first, last)
    high, low = split(uf)
    uf_ref[:, cols] = uf
    uh[:, cols] = high
    ul[:, cols] = low
    turned = uf.T
    high, low = split(turned)
    uth[cols, :] = high
    utl[cols, :] = low


def block_held(stratum, rank):
    return rank ^ (2 if stratum % 2 else 0)


def group_rows(rank):
    return [pl.ds(pl.multiple_of((rank ^ k) * 64, 64), 64) for k in (0, 2, 1, 3)]


def offer_kernel(rank, count, user, item, users, items, accum, out, counts):
    for s in range(STRATA):
        for k in range(32):
            counts[s, k] = 0.0
        for p in range(SLOTS):
            slot = s * SLOTS + p
            where = user[0, slot] * 4 + item[0, slot]
            counts[s, where] += jnp.where(p < count[0, s], 1.0, 0.0)
    out[:, :1024] = users[...]
    for k, source in enumerate((items, accum)):
        for j in range(2):
            start = 1024 + (2 * k + j) * EDGE
            out[:, start : start + EDGE] = block_of(source, rank[0] ^ 2 ^ j)


def offer(rank, count, user, item, users, items, accum):
    return pl.pallas_call(
        offer_kernel,
        out_shape=(struct(64, 1536), struct(STRATA, 32)),
        in_specs=[SMEM] * 4 + [VMEM] * 3,
        out_specs=(VMEM, SMEM),
        compiler_params=PARAMS,
        cost_estimate=cost(2),
        name="offer",
    )(rank, count, user, item, users, items, accum)


def pack_kernel(rank, users, items, accum, pair, out):
    sibling = rank[0] ^ 1
    out[0, :, :1024] = users[...]
    out[1, :, :1024] = pair[:, :1024]
    for k, source in enumerate((items, accum)):
        cols = slice(1024 + k * EDGE, 1024 + (k + 1) * EDGE)
        out[0, :, cols] = block_of(source, sibling)
        start = 1024 + (2 * k + 1) * EDGE
        out[1, :, cols] = pair[:, start : start + EDGE]


def pack(rank, users, items, accum, pair):
    return pl.pallas_call(
        pack_kernel,
        out_shape=struct(2, 64, 1280),
        in_specs=[SMEM] + [VMEM] * 4,
        out_specs=VMEM,
        compiler_params=PARAMS,
        cost_estimate=cost(0),
        name="pack",
    )(rank, users, items, accum, pair)


def prepare_kernel(
    rank, own, items, accum, pair, sib, uf, uh, ul, uth, utl, state, users
):
    mine = rank[0]
    places = group_rows(mine)
    parts = (own, pair.at[:, :1024], sib.at[0, :, :1024], sib.at[1, :, :1024])
    for place, part in zip(places, parts):
        users[place, :] = part[...]
    for first in range(0, 1024, CHUNK):
        last = first + CHUNK
        store_users(users[:, first:last], first, last, uf, uh, ul, uth, utl)
    for k, own_part in enumerate((items, accum)):
        state[k, places[0], :] = block_of(own_part, mine)
        start = 1024 + 2 * k * EDGE
        state[k, places[1], :] = pair[:, start : start + EDGE]
        for j in range(2):
            start = 1024 + EDGE * k
            state[k, places[2 + j], :] = sib[j, :, start : start + EDGE]


USER_SHAPES = (
    struct(256, 1024),
    struct(256, 1024, dtype=BF16),
    struct(256, 1024, dtype=BF16),
    struct(1024, 256, dtype=BF16),
    struct(1024, 256, dtype=BF16),
)


def prepare(rank, own, items, accum, pair, sib):
    return pl.pallas_call(
        prepare_kernel,
        out_shape=USER_SHAPES + (struct(2, 256, EDGE),),
        in_specs=[SMEM] + [VMEM] * 5,
        out_specs=(VMEM,) * 6,
        scratch_shapes=[pltpu.VMEM((256, 1024), F32)],
        compiler_params=PARAMS,
        cost_estimate=cost(0),
        name="prepare",
    )(rank, own, items, accum, pair, sib)


def add_tile(rank, place, pieces, top, sums):
    spans = [
        pl.ds(pl.multiple_of(top + (rank ^ k) * QUARTER, QUARTER), QUARTER)
        for k in (0, 2, 1, 3)
    ]
    added = [sums[span, :] + piece[place].astype(F32) for span, piece in zip(spans, pieces)]
    for span, value in zip(spans, added):
        sums[span, :] = value


def sum_kernel(stratum, rank, count, user, item, *rest):
    pieces, sums = rest[:4], rest[4]
    mine = rank[0]
    sums[...] = jnp.zeros_like(sums)
    for p in range(SLOTS):
        slot = stratum * SLOTS + p

        @pl.when(p < count[0, stratum])
        def _():
            target = sums.at[item[0, slot] ^ block_held(stratum, mine)]
            add_tile(mine, p, pieces, user[0, slot] * EDGE, target)


def sum_tiles(stratum, scalars, pieces):
    return pl.pallas_call(
        functools.partial(sum_kernel, stratum),
        out_shape=struct(4, 1024, EDGE),
        in_specs=[SMEM] * 4 + [VMEM] * 4,
        out_specs=VMEM,
        compiler_params=PARAMS,
        cost_estimate=cost(30 if stratum == 0 else 0),
        name=f"sum_tiles{stratum}",
    )(*scalars[:4], *pieces)


def item_kernel(stratum, rank, counts, uh, ul, uth, utl, state, sums, *rest):
    *outs, errors = rest
    mine = rank[0]
    items = state[0]
    vh, vl = split(items)
    both = jnp.concatenate([vh, vl], axis=1)
    grad = jnp.zeros_like(items)
    for first in range(0, 1024, CHUNK):
        rows = slice(first, first + CHUNK)
        wide = dot(uth[rows, :], both)
        predicted = wide[:, :EDGE] + wide[:, EDGE:] + dot(utl[rows, :], vh)
        parts = []
        for k in range(CHUNK // EDGE):
            top = first + k * EDGE
            live = counts[stratum, top // EDGE * 4 + block_held(stratum, mine)]
            parts.append(sums[0, top : top + EDGE, :] - live * predicted[k * EDGE : (k + 1) * EDGE])
        eh, el = split(jnp.concatenate(parts, axis=0))
        es = jnp.concatenate([eh, el], axis=1)
        errors[rows, :] = es
        wide = dot(uh[:, rows], es)
        grad += wide[:, :EDGE] + wide[:, EDGE:] + dot(ul[:, rows], eh)
    grad = grad - DECAY * items
    accum = state[1] + grad * grad
    items = items + LR_ITEM * grad / jnp.sqrt(accum)
    if stratum < STRATA - 1:
        outs[0][0] = items
        outs[0][1] = accum
    else:
        near, far, spot = outs
        spot[0] = items
        spot[1] = accum
        for j, rows in enumerate(group_rows(mine)):
            target = far if j % 2 else near
            for k in range(2):
                target[j // 2, k] = spot[k, rows, :]


def item_step(stratum, scalars, users, state, sums):
    if stratum < STRATA - 1:
        out = (struct(2, 256, EDGE),)
    else:
        out = (struct(2, 2, 64, EDGE), struct(2, 2, 64, EDGE), struct(2, 256, EDGE))
    return pl.pallas_call(
        functools.partial(item_kernel, stratum),
        out_shape=out + (struct(1024, 2 * EDGE, dtype=BF16),),
        in_specs=[SMEM] * 2 + [VMEM] * 6,
        out_specs=(VMEM,) * (len(out) + 1),
        compiler_params=PARAMS,
        cost_estimate=cost(12),
        name=f"item_step{stratum}",
    )(scalars[0], scalars[4], *users[1:], state, sums)


def user_kernel(stratum, rank, counts, uf, uth, utl, v, vp, vs, vd, errors, sums, *outs):
    mine = rank[0]
    last = stratum == STRATA - 1
    others = jnp.concatenate([vp[...], vs[...], vd[...]], axis=1)
    oh, ol = split(others)
    if last:
        rows = pl.ds(pl.multiple_of(mine * 64, 64), 64)
        kept = jnp.concatenate([x[rows, :] for x in (v, vp, vs, vd)], axis=1)
        kh, kl = split(kept)
    else:
        rows = slice(None)
        vh, vl = split(v[...])
        kh = jnp.concatenate([vh, oh], axis=1)
        kl = jnp.concatenate([vl, ol], axis=1)
    for first in range(0, 1024, CHUNK):
        span = slice(first, first + CHUNK)
        predicted = three(dot, (uth[span, :], utl[span, :]), (oh, ol))
        lines = []
        for k in range(CHUNK // EDGE):
            top = first + k * EDGE
            line = []
            for j, other in enumerate((2, 1, 3)):
                live = counts[stratum, top // EDGE * 4 + (block_held(stratum, mine) ^ other)]
                part = predicted[k * EDGE : (k + 1) * EDGE, j * EDGE : (j + 1) * EDGE]
                line.append(sums[other, top : top + EDGE, :] - live * part)
            lines.append(jnp.concatenate(line, axis=1))
        eh, el = split(jnp.concatenate(lines, axis=0))
        eh = jnp.concatenate([errors[span, :EDGE], eh], axis=1)
        el = jnp.concatenate([errors[span, EDGE:], el], axis=1)
        grad = three(dot_nt, (kh, kl), (eh, el))
        old = uf[rows, span]
        new = old + LR_USER * (grad - DECAY * old)
        if last:
            outs[0][:, span] = new
        else:
            store_users(new, first, first + CHUNK, *outs)


def user_step(stratum, scalars, users, v, others, errors, sums):
    last = stratum == STRATA - 1
    return pl.pallas_call(
        functools.partial(user_kernel, stratum),
        out_shape=(struct(64, 1024),) if last else USER_SHAPES,
        in_specs=[SMEM] * 2 + [VMEM] * 9,
        out_specs=(VMEM,) * (1 if last else 5),
        compiler_params=PARAMS,
        cost_estimate=cost(0),
        name=f"user_step{stratum}",
    )(scalars[0], scalars[4], users[0], users[3], users[4], v, *others, errors, sums)


def place_kernel(rank, near, far, other, items, accum):
    mine = rank[0]
    for k, part in enumerate((near.at[0], other.at[0], far.at[0], other.at[1])):
        cols = pl.ds(pl.multiple_of((mine ^ k ^ 2) * EDGE, EDGE), EDGE)
        items[:, cols] = part[0]
        accum[:, cols] = part[1]


def place_state(rank, near, far, other):
    return pl.pallas_call(
        place_kernel,
        out_shape=(struct(64, 512), struct(64, 512)),
        in_specs=[SMEM] + [VMEM] * 3,
        out_specs=(VMEM, VMEM),
        compiler_params=PARAMS,
        cost_estimate=cost(2),
        name="place_state",
    )(rank, near, far, other)


def exchange(x, by):
    return lax.ppermute(x, "rank", [(r, r ^ by) for r in range(4)])


def exchange_halves(x):
    return jnp.concatenate([exchange(x[:128], 1), exchange(x[128:], 1)])


def send_on(x, by):
    n = lax.axis_size("blk")
    return lax.ppermute(
        x,
        ("blk", "rank"),
        [(o * 4 + r, (o + 1) % n * 4 + (r ^ by)) for o in range(n) for r in range(4)],
    )


def body(
    ratings,
    send_list,
    plan,
    block_count,
    block_user,
    block_item,
    user_factors,
    item_factors,
    item_accum,
):
    rank = lax.axis_index("rank").astype(jnp.int32).reshape(1)
    quarter = (user_factors, item_factors, item_accum)
    offered, counts = offer(rank, block_count, block_user, block_item, *quarter)
    pair = exchange(offered, 2)
    scalars = (rank, block_count, block_user, block_item, counts)

    outgoing = gather_outgoing(rank, send_list, ratings)
    received = lax.all_to_all(outgoing, "blk", split_axis=0, concat_axis=0, tiled=True)

    tiles = list(order_received(plan, received))
    first = tiles[0]
    first_pair = exchange(first, 2)
    first_sib = exchange(first, 1)

    pair, tiles[2] = lax.optimization_barrier((pair, tiles[2]))
    sib = exchange(pack(rank, *quarter, pair), 1)
    *users, state = prepare(rank, *quarter, pair, sib)

    tiles[1], first_pair = lax.optimization_barrier((tiles[1], first_pair))
    next_pair = exchange(tiles[1], 2)
    sums = sum_tiles(0, scalars, (first, first_pair, first_sib, exchange(first_pair, 1)))
    for stratum in range(STRATA):
        last = stratum == STRATA - 1
        *out, errors = item_step(stratum, scalars, users, state, sums)
        v = state[0]
        vp = exchange(v, 2)
        if last:
            near = send_on(out[0], 0)
            far = send_on(out[1], 2)
            late, errors = lax.optimization_barrier((v, errors))
        else:
            state = send_on(out[0], 2)
            late, own, errors = lax.optimization_barrier((v, tiles[stratum + 1], errors))
            next_sib = exchange(own, 1)
            next_pair, errors = lax.optimization_barrier((next_pair, errors))
            next_diag = exchange(next_pair, 1)
        if last:
            late, vp, errors = lax.optimization_barrier((late, vp, errors))
            vs, vd = exchange_halves(late), exchange_halves(vp)
        else:
            vs = exchange(late, 1)
            vp, errors = lax.optimization_barrier((vp, errors))
            vd = exchange(vp, 1)
        if not last:
            after = (tiles[stratum + 1], next_pair, next_sib, next_diag)
            if stratum < 2:
                tiles[stratum + 2], vd = lax.optimization_barrier((tiles[stratum + 2], vd))
                next_pair = exchange(tiles[stratum + 2], 2)
            vs, vd, after, errors = lax.optimization_barrier((vs, vd, after, errors))
        else:
            vs, vd, errors = lax.optimization_barrier((vs, vd, errors))
        users = user_step(stratum, scalars, users, v, (vp, vs, vd), errors, sums)
        if not last:
            sums = sum_tiles(stratum + 1, scalars, after)
            state, users, sums = lax.optimization_barrier((state, users, sums))
    near, far, users_out = lax.optimization_barrier((near, far, users[0]))
    other = exchange(jnp.stack([near[1], far[1]]), 1)
    items_out, accum_out = place_state(rank, near, far, other)
    return users_out, items_out, accum_out


def solution(mesh):
    placed = (
        P("blk", None, None),
        P("blk", None),
        P("blk", None),
        P("blk", None),
        P("blk", None),
        P("blk", None),
        P("rank", "blk"),
        P("rank", "blk"),
        P("rank", "blk"),
    )
    return jax.shard_map(
        body,
        mesh=mesh,
        in_specs=placed,
        out_specs=(P("rank", "blk"), P("rank", "blk"), P("rank", "blk")),
        check_vma=False,
    )
```

```python
import functools

import jax
import jax.numpy as jnp
from jax import lax
from jax.experimental import pallas as pl
from jax.experimental.pallas import tpu as pltpu
from jax.sharding import PartitionSpec as P

LR_USER = 0.01
LR_ITEM = 0.05
DECAY = 0.05
F32 = jnp.float32
BF16 = jnp.bfloat16
EDGE = 128
SLOTS = 16
STRATA = 4
QUARTER = 32
CHUNK = 1024
VMEM = pl.BlockSpec(memory_space=pltpu.VMEM)
SMEM = pl.BlockSpec(memory_space=pltpu.SMEM)
HBM = pl.BlockSpec(memory_space=pltpu.HBM)
PARAMS = pltpu.CompilerParams(vmem_limit_bytes=16 * 2**20)


def cost(time):
    return pl.CostEstimate(flops=10**9 * time, bytes_accessed=3 * 10**6 * time, transcendentals=0)


def split(x):
    high = x.astype(BF16)
    return high, (x - high.astype(F32)).astype(BF16)


def dot(a, b):
    return jnp.dot(a, b, preferred_element_type=F32)


def dot_nt(a, b):
    return lax.dot_general(a, b, (((1,), (1,)), ((), ())), preferred_element_type=F32)


def three(product, a, b):
    return product(a[0], b[0]) + product(a[0], b[1]) + product(a[1], b[0])


def struct(*shape, dtype=F32):
    return jax.ShapeDtypeStruct(shape, dtype)


def gather_kernel(rank, routes, ratings, out, places, sems):
    fetch = pltpu.make_async_copy(routes, places, sems.at[0])
    fetch.start()
    fetch.wait()
    row = pl.multiple_of(rank[0] * QUARTER, QUARTER)
    for d in range(64):
        pltpu.make_async_copy(
            ratings.at[places[0, d], pl.ds(row, QUARTER), :], out.at[d], sems.at[1]
        ).start()
    pltpu.make_async_copy(out, out, sems.at[1]).wait()


def gather_outgoing(rank, routes, ratings):
    return pl.pallas_call(
        gather_kernel,
        out_shape=struct(64, QUARTER, EDGE, dtype=BF16),
        in_specs=[SMEM, HBM, HBM],
        out_specs=VMEM,
        scratch_shapes=[pltpu.SMEM((1, 64), jnp.int32), pltpu.SemaphoreType.DMA((2,))],
        compiler_params=pltpu.CompilerParams(vmem_limit_bytes=65 * 10**6),
        cost_estimate=cost(2),
        name="gather_outgoing",
    )(rank, routes, ratings)


def order_kernel(plan, received, *outs):
    for stratum, out in enumerate(outs):
        for p in range(SLOTS):
            out[p] = received[plan[0, stratum * SLOTS + p]]


def order_received(plan, received):
    return pl.pallas_call(
        order_kernel,
        out_shape=(struct(SLOTS, QUARTER, EDGE, dtype=BF16),) * STRATA,
        in_specs=[SMEM, VMEM],
        out_specs=(VMEM,) * STRATA,
        compiler_params=PARAMS,
        cost_estimate=cost(4),
        name="order_received",
    )(plan, received)


def block_of(ref, block):
    return ref[:, pl.ds(pl.multiple_of(block * EDGE, EDGE), EDGE)]


def store_users(uf, first, last, uf_ref, uh, ul, uth, utl):
    cols = slice(first, last)
    high, low = split(uf)
    uf_ref[:, cols] = uf
    uh[:, cols] = high
    ul[:, cols] = low
    turned = uf.T
    high, low = split(turned)
    uth[cols, :] = high
    utl[cols, :] = low


def block_held(stratum, rank):
    return rank ^ (2 if stratum % 2 else 0)


def group_rows(rank):
    return [pl.ds(pl.multiple_of((rank ^ k) * 64, 64), 64) for k in (0, 2, 1, 3)]


def offer_kernel(rank, count, user, item, users, items, accum, out, counts):
    for s in range(STRATA):
        for k in range(32):
            counts[s, k] = 0.0
        for p in range(SLOTS):
            slot = s * SLOTS + p
            where = user[0, slot] * 4 + item[0, slot]
            counts[s, where] += jnp.where(p < count[0, s], 1.0, 0.0)
    out[:, :1024] = users[...]
    for k, source in enumerate((items, accum)):
        for j in range(2):
            start = 1024 + (2 * k + j) * EDGE
            out[:, start : start + EDGE] = block_of(source, rank[0] ^ 2 ^ j)


def offer(rank, count, user, item, users, items, accum):
    return pl.pallas_call(
        offer_kernel,
        out_shape=(struct(64, 1536), struct(STRATA, 32)),
        in_specs=[SMEM] * 4 + [VMEM] * 3,
        out_specs=(VMEM, SMEM),
        compiler_params=PARAMS,
        cost_estimate=cost(2),
        name="offer",
    )(rank, count, user, item, users, items, accum)


def pack_kernel(rank, users, items, accum, pair, out):
    sibling = rank[0] ^ 1
    out[0, :, :1024] = users[...]
    out[1, :, :1024] = pair[:, :1024]
    for k, source in enumerate((items, accum)):
        cols = slice(1024 + k * EDGE, 1024 + (k + 1) * EDGE)
        out[0, :, cols] = block_of(source, sibling)
        start = 1024 + (2 * k + 1) * EDGE
        out[1, :, cols] = pair[:, start : start + EDGE]


def pack(rank, users, items, accum, pair):
    return pl.pallas_call(
        pack_kernel,
        out_shape=struct(2, 64, 1280),
        in_specs=[SMEM] + [VMEM] * 4,
        out_specs=VMEM,
        compiler_params=PARAMS,
        cost_estimate=cost(0),
        name="pack",
    )(rank, users, items, accum, pair)


def prepare_kernel(
    rank, own, items, accum, pair, sib, uf, uh, ul, uth, utl, state, users
):
    mine = rank[0]
    places = group_rows(mine)
    parts = (own, pair.at[:, :1024], sib.at[0, :, :1024], sib.at[1, :, :1024])
    for place, part in zip(places, parts):
        users[place, :] = part[...]
    for first in range(0, 1024, CHUNK):
        last = first + CHUNK
        store_users(users[:, first:last], first, last, uf, uh, ul, uth, utl)
    for k, own_part in enumerate((items, accum)):
        state[k, places[0], :] = block_of(own_part, mine)
        start = 1024 + 2 * k * EDGE
        state[k, places[1], :] = pair[:, start : start + EDGE]
        for j in range(2):
            start = 1024 + EDGE * k
            state[k, places[2 + j], :] = sib[j, :, start : start + EDGE]


USER_SHAPES = (
    struct(256, 1024),
    struct(256, 1024, dtype=BF16),
    struct(256, 1024, dtype=BF16),
    struct(1024, 256, dtype=BF16),
    struct(1024, 256, dtype=BF16),
)


def prepare(rank, own, items, accum, pair, sib):
    return pl.pallas_call(
        prepare_kernel,
        out_shape=USER_SHAPES + (struct(2, 256, EDGE),),
        in_specs=[SMEM] + [VMEM] * 5,
        out_specs=(VMEM,) * 6,
        scratch_shapes=[pltpu.VMEM((256, 1024), F32)],
        compiler_params=PARAMS,
        cost_estimate=cost(0),
        name="prepare",
    )(rank, own, items, accum, pair, sib)


def add_tile(rank, place, live, pieces, top, sums):
    spans = [
        pl.ds(pl.multiple_of(top + (rank ^ k) * QUARTER, QUARTER), QUARTER)
        for k in (0, 2, 1, 3)
    ]
    added = [
        sums[span, :] + jnp.where(live, piece[place].astype(F32), 0.0)
        for span, piece in zip(spans, pieces)
    ]
    for span, value in zip(spans, added):
        sums[span, :] = value


def sum_kernel(stratum, rank, count, user, item, *rest):
    pieces, sums = rest[:4], rest[4]
    mine = rank[0]
    sums[...] = jnp.zeros_like(sums)
    for p in range(SLOTS):
        slot = stratum * SLOTS + p
        live = p < count[0, stratum]
        target = sums.at[item[0, slot] ^ block_held(stratum, mine)]
        add_tile(mine, p, live, pieces, user[0, slot] * EDGE, target)


def sum_tiles(stratum, scalars, pieces):
    return pl.pallas_call(
        functools.partial(sum_kernel, stratum),
        out_shape=struct(4, 1024, EDGE),
        in_specs=[SMEM] * 4 + [VMEM] * 4,
        out_specs=VMEM,
        compiler_params=PARAMS,
        cost_estimate=cost(30 if stratum == 0 else 0),
        name=f"sum_tiles{stratum}",
    )(*scalars[:4], *pieces)


def item_kernel(stratum, rank, counts, uh, ul, uth, utl, state, sums, *rest):
    *outs, errors = rest
    mine = rank[0]
    items = state[0]
    vh, vl = split(items)
    both = jnp.concatenate([vh, vl], axis=1)
    grad = jnp.zeros_like(items)
    for first in range(0, 1024, CHUNK):
        rows = slice(first, first + CHUNK)
        wide = dot(uth[rows, :], both)
        predicted = wide[:, :EDGE] + wide[:, EDGE:] + dot(utl[rows, :], vh)
        parts = []
        for k in range(CHUNK // EDGE):
            top = first + k * EDGE
            live = counts[stratum, top // EDGE * 4 + block_held(stratum, mine)]
            parts.append(sums[0, top : top + EDGE, :] - live * predicted[k * EDGE : (k + 1) * EDGE])
        eh, el = split(jnp.concatenate(parts, axis=0))
        es = jnp.concatenate([eh, el], axis=1)
        errors[rows, :] = es
        wide = dot(uh[:, rows], es)
        grad += wide[:, :EDGE] + wide[:, EDGE:] + dot(ul[:, rows], eh)
    grad = grad - DECAY * items
    accum = state[1] + grad * grad
    items = items + LR_ITEM * grad / jnp.sqrt(accum)
    if stratum < STRATA - 1:
        outs[0][0] = items
        outs[0][1] = accum
    else:
        near, far, spot = outs
        spot[0] = items
        spot[1] = accum
        for j, rows in enumerate(group_rows(mine)):
            target = far if j % 2 else near
            for k in range(2):
                target[j // 2, k] = spot[k, rows, :]


def item_step(stratum, scalars, users, state, sums):
    if stratum < STRATA - 1:
        out = (struct(2, 256, EDGE),)
    else:
        out = (struct(2, 2, 64, EDGE), struct(2, 2, 64, EDGE), struct(2, 256, EDGE))
    return pl.pallas_call(
        functools.partial(item_kernel, stratum),
        out_shape=out + (struct(1024, 2 * EDGE, dtype=BF16),),
        in_specs=[SMEM] * 2 + [VMEM] * 6,
        out_specs=(VMEM,) * (len(out) + 1),
        compiler_params=PARAMS,
        cost_estimate=cost(12),
        name=f"item_step{stratum}",
    )(scalars[0], scalars[4], *users[1:], state, sums)


def user_kernel(stratum, rank, counts, uf, uth, utl, v, vp, vs, vd, errors, sums, *outs):
    mine = rank[0]
    last = stratum == STRATA - 1
    others = jnp.concatenate([vp[...], vs[...], vd[...]], axis=1)
    oh, ol = split(others)
    if last:
        rows = pl.ds(pl.multiple_of(mine * 64, 64), 64)
        kept = jnp.concatenate([x[rows, :] for x in (v, vp, vs, vd)], axis=1)
        kh, kl = split(kept)
    else:
        rows = slice(None)
        vh, vl = split(v[...])
        kh = jnp.concatenate([vh, oh], axis=1)
        kl = jnp.concatenate([vl, ol], axis=1)
    for first in range(0, 1024, CHUNK):
        span = slice(first, first + CHUNK)
        predicted = three(dot, (uth[span, :], utl[span, :]), (oh, ol))
        lines = []
        for k in range(CHUNK // EDGE):
            top = first + k * EDGE
            line = []
            for j, other in enumerate((2, 1, 3)):
                live = counts[stratum, top // EDGE * 4 + (block_held(stratum, mine) ^ other)]
                part = predicted[k * EDGE : (k + 1) * EDGE, j * EDGE : (j + 1) * EDGE]
                line.append(sums[other, top : top + EDGE, :] - live * part)
            lines.append(jnp.concatenate(line, axis=1))
        eh, el = split(jnp.concatenate(lines, axis=0))
        eh = jnp.concatenate([errors[span, :EDGE], eh], axis=1)
        el = jnp.concatenate([errors[span, EDGE:], el], axis=1)
        grad = three(dot_nt, (kh, kl), (eh, el))
        old = uf[rows, span]
        new = old + LR_USER * (grad - DECAY * old)
        if last:
            outs[0][:, span] = new
        else:
            store_users(new, first, first + CHUNK, *outs)


def user_step(stratum, scalars, users, v, others, errors, sums):
    last = stratum == STRATA - 1
    return pl.pallas_call(
        functools.partial(user_kernel, stratum),
        out_shape=(struct(64, 1024),) if last else USER_SHAPES,
        in_specs=[SMEM] * 2 + [VMEM] * 9,
        out_specs=(VMEM,) * (1 if last else 5),
        compiler_params=PARAMS,
        cost_estimate=cost(0),
        name=f"user_step{stratum}",
    )(scalars[0], scalars[4], users[0], users[3], users[4], v, *others, errors, sums)


def place_kernel(rank, near, far, other, items, accum):
    mine = rank[0]
    for k, part in enumerate((near.at[0], other.at[0], far.at[0], other.at[1])):
        cols = pl.ds(pl.multiple_of((mine ^ k ^ 2) * EDGE, EDGE), EDGE)
        items[:, cols] = part[0]
        accum[:, cols] = part[1]


def place_state(rank, near, far, other):
    return pl.pallas_call(
        place_kernel,
        out_shape=(struct(64, 512), struct(64, 512)),
        in_specs=[SMEM] + [VMEM] * 3,
        out_specs=(VMEM, VMEM),
        compiler_params=PARAMS,
        cost_estimate=cost(2),
        name="place_state",
    )(rank, near, far, other)


def exchange(x, by):
    return lax.ppermute(x, "rank", [(r, r ^ by) for r in range(4)])


def exchange_halves(x):
    return jnp.concatenate([exchange(x[:128], 1), exchange(x[128:], 1)])


def send_on(x, by):
    n = lax.axis_size("blk")
    return lax.ppermute(
        x,
        ("blk", "rank"),
        [(o * 4 + r, (o + 1) % n * 4 + (r ^ by)) for o in range(n) for r in range(4)],
    )


def body(
    ratings,
    send_list,
    plan,
    block_count,
    block_user,
    block_item,
    user_factors,
    item_factors,
    item_accum,
):
    rank = lax.axis_index("rank").astype(jnp.int32).reshape(1)
    quarter = (user_factors, item_factors, item_accum)
    offered, counts = offer(rank, block_count, block_user, block_item, *quarter)
    pair = exchange(offered, 2)
    scalars = (rank, block_count, block_user, block_item, counts)

    outgoing = gather_outgoing(rank, send_list, ratings)
    received = lax.all_to_all(outgoing, "blk", split_axis=0, concat_axis=0, tiled=True)

    tiles = list(order_received(plan, received))
    first = tiles[0]
    first_pair = exchange(first, 2)
    first_sib = exchange(first, 1)

    pair, tiles[2] = lax.optimization_barrier((pair, tiles[2]))
    sib = exchange(pack(rank, *quarter, pair), 1)
    *users, state = prepare(rank, *quarter, pair, sib)

    tiles[1], first_pair = lax.optimization_barrier((tiles[1], first_pair))
    next_pair = exchange(tiles[1], 2)
    sums = sum_tiles(0, scalars, (first, first_pair, first_sib, exchange(first_pair, 1)))
    for stratum in range(STRATA):
        last = stratum == STRATA - 1
        *out, errors = item_step(stratum, scalars, users, state, sums)
        v = state[0]
        vp = exchange(v, 2)
        if last:
            near = send_on(out[0], 0)
            far = send_on(out[1], 2)
            late, errors = lax.optimization_barrier((v, errors))
        else:
            state = send_on(out[0], 2)
            late, own, errors = lax.optimization_barrier((v, tiles[stratum + 1], errors))
            next_sib = exchange(own, 1)
            next_pair, errors = lax.optimization_barrier((next_pair, errors))
            next_diag = exchange(next_pair, 1)
        if last:
            late, vp, errors = lax.optimization_barrier((late, vp, errors))
            vs, vd = exchange_halves(late), exchange_halves(vp)
        else:
            vs = exchange(late, 1)
            vp, errors = lax.optimization_barrier((vp, errors))
            vd = exchange(vp, 1)
        if not last:
            after = (tiles[stratum + 1], next_pair, next_sib, next_diag)
            if stratum < 2:
                tiles[stratum + 2], vd = lax.optimization_barrier((tiles[stratum + 2], vd))
                next_pair = exchange(tiles[stratum + 2], 2)
            vs, vd, after, errors = lax.optimization_barrier((vs, vd, after, errors))
        else:
            vs, vd, errors = lax.optimization_barrier((vs, vd, errors))
        users = user_step(stratum, scalars, users, v, (vp, vs, vd), errors, sums)
        if not last:
            sums = sum_tiles(stratum + 1, scalars, after)
            state, users, sums = lax.optimization_barrier((state, users, sums))
    near, far, users_out = lax.optimization_barrier((near, far, users[0]))
    other = exchange(jnp.stack([near[1], far[1]]), 1)
    items_out, accum_out = place_state(rank, near, far, other)
    return users_out, items_out, accum_out


def solution(mesh):
    placed = (
        P("blk", None, None),
        P("blk", None),
        P("blk", None),
        P("blk", None),
        P("blk", None),
        P("blk", None),
        P("rank", "blk"),
        P("rank", "blk"),
        P("rank", "blk"),
    )
    return jax.shard_map(
        body,
        mesh=mesh,
        in_specs=placed,
        out_specs=(P("rank", "blk"), P("rank", "blk"), P("rank", "blk")),
        check_vma=False,
    )
```
